1024 devices in a mesh: depth: 64 (over x_hi, z, core), chan: 16 (over y, x_lo).
Axes of the slice: x: 4 (x_hi: 2, x_lo: 2; x = x_hi * 2 + x_lo), y: 8, z: 16, core: 2. Of those that a mesh axis runs over, the one named last changes fastest.
Arguments:
- activations: bfloat16 [64, 64, 32, 128], P('chan', 'depth'), may hold values from -6 to 6
- slopes: bfloat16 [128, 64, 32, 128], P('chan', 'depth'), may hold values from -6 to 6
- weight: bfloat16 [27, 64, 128], replicated, may hold values from -0.15625 to 0.15625
Outputs:
- inputs_grad: bfloat16 [64, 64, 32, 128], P('chan', 'depth')
- weight_grad: float32 [27, 64, 128], P(None, None, 'chan')
The draws below stay inside these ranges and needn't reach their ends.
All inputs are finite; a program needn't handle non-finite values.
Results may differ from the reference program's by a relative error of at most 0.0015.
Values may be sent and summed in bfloat16 or wider, within the bound.
A program may use at most 32 MiB of HBM per device.

```python
import math
import jax
import jax.numpy as jnp
from jax import lax

CIN = 64
COUT = 128
HROWS = 32
WCOLS = 128
DEPTH = 64


def block_scale(own_key, shape, shards, least, top_value):
    gain, own = 1.0, jax.random.fold_in(own_key, 6)
    for axis_at, parts in shards:
        heights = jnp.exp(jax.random.uniform(jax.random.fold_in(own, axis_at), (parts,), jnp.float32, least / len(shards), top_value / len(shards)))
        gain = gain * jnp.repeat(heights, shape[axis_at] // parts).reshape([-1 if axis == axis_at else 1 for axis in range(len(shape))])
    return gain


def scatter_about(own_key, shape, width, bound, pieces=(), dtype=jnp.bfloat16):
    drawn = width * jax.random.normal(own_key, shape, jnp.float32)
    if pieces:
        drawn = drawn * block_scale(own_key, shape, pieces, -0.22, 0.18)
    return jnp.clip(drawn, -bound, bound).astype(dtype)


def setup_inputs(seed: int = 0) -> dict:
    key_of = jax.random.split(jax.random.key(seed), 4)
    return {
        "activations": scatter_about(key_of[0], (CIN, DEPTH, HROWS, WCOLS), 1.0, 6.0, ((0, 16), (1, 64))),
        "slopes": scatter_about(key_of[1], (COUT, DEPTH, HROWS, WCOLS), 1.0, 6.0, ((0, 16), (1, 64))),
        "weight": scatter_about(key_of[2], (27, CIN, COUT), (27 * CIN) ** -0.5, 0.15625),
    }


def reference(activations, slopes, weight):
    inputs = activations.astype(jnp.float32)
    grads = slopes.astype(jnp.float32)
    filt = weight.astype(jnp.float32)
    kernel = filt.reshape(3, 3, 3, CIN, COUT)[::-1, ::-1, ::-1]
    inputs_grad = lax.conv_general_dilated(grads[None], kernel, (1, 1, 1), ((1, 1), (1, 1), (1, 1)), dimension_numbers=('NCDHW', 'DHWOI', 'NCDHW'), precision=lax.Precision.HIGHEST)[0]
    padded = jnp.pad(inputs, ((0, 0), (1, 1), (1, 1), (1, 1)))
    flat_grads = grads.reshape(COUT, -1)
    scaling = 1.0 / math.sqrt(DEPTH * HROWS * WCOLS)
    taps = []
    for first in range(3):
        for second in range(3):
            for third in range(3):
                window = padded[:, first:first + DEPTH, second:second + HROWS, third:third + WCOLS].reshape(CIN, -1)
                taps.append(lax.dot_general(window, flat_grads, (((1,), (1,)), ((), ())), precision=lax.Precision.HIGHEST))
    weight_grad = jnp.stack(taps, 0) * scaling
    return (inputs_grad.astype(jnp.bfloat16), weight_grad)
```

```python
import math

import jax
import jax.numpy as jnp
from jax import lax
from jax.experimental import pallas as pl
from jax.experimental.pallas import tpu as pltpu
from jax.sharding import PartitionSpec as P

MESH = pl.DeviceIdType.MESH
F32, BF16 = jnp.float32, jnp.bfloat16
ND, NC = 64, 16
NZ = 16
PIECES = 56


def far_first():
    offsets = [(xh, dz, k) for xh in range(2) for dz in range(NZ) for k in range(2)]
    offsets.sort(key=lambda o: -(20 * o[0] + 10 * min(o[1], NZ - o[1]) + o[2]))
    return offsets[:-1]


DEPTH_OFFSETS = far_first()
CHAN_OFFSETS = (8, 9, 6, 10, 7, 11, 4, 12, 5, 13, 2, 14, 3, 15, 1)


def moved(d, offset):
    xh, dz, k = offset
    z = lax.rem(lax.rem(d // 2, NZ) + dz, NZ)
    return ((d // 32) ^ xh) * 32 + z * 2 + (lax.rem(d, 2) ^ k)


def owned(d):
    return d - d // 8


def owns(d):
    return lax.rem(d, 8) != 7


def drained(ref, sem):
    pltpu.make_async_copy(ref, ref, sem).wait()


def kernel(
    act_in, slopes_in, weight_in,
    grad_out, filt_out,
    act_all, slopes_all, weight_v, slopes_f, act_f, taps, act_taps,
    rows_send, rows_recv, rows_taps, near_send, near_recv, back_send, back_recv,
    piece_send, piece_recv, piece_sum, gathered, spread,
    local_sem, send_sem, recv_sem,
):
    d, c = lax.axis_index("depth"), lax.axis_index("chan")
    y, x = c // 2, lax.rem(c, 2)
    up, down = lax.rem(d + 1, ND), lax.rem(d + ND - 1, ND)
    other = c ^ 1

    loads = [
        pltpu.make_async_copy(slopes_in, slopes_all.at[2 + x], local_sem.at[0]),
        pltpu.make_async_copy(act_in, act_all.at[y], local_sem.at[1]),
        pltpu.make_async_copy(weight_in, weight_v, local_sem.at[2]),
    ]
    for load in loads:
        load.start()

    depth_peers = [(moved(d, o), c) for o in DEPTH_OFFSETS]
    chan_peers = [(d, lax.rem(c + k, NC)) for k in CHAN_OFFSETS]
    diagonal = [(up, other), (down, other)]
    greeted = depth_peers + chan_peers + diagonal
    barrier = pltpu.get_barrier_semaphore()
    for peer in greeted:
        pl.semaphore_signal(barrier, inc=1, device_id=peer, device_id_type=MESH)

    def send(src, dst, group, peer):
        pltpu.make_async_remote_copy(
            src_ref=src, dst_ref=dst, send_sem=send_sem.at[group],
            recv_sem=recv_sem.at[group], device_id=peer, device_id_type=MESH,
        ).start()

    lane = lax.broadcasted_iota(jnp.int32, (16, 128), 1)

    loads[0].wait()
    slopes_f[0:256] = slopes_all[2 + x].astype(F32)
    zero8 = jnp.zeros((8, 128), F32)

    def own_row(h):
        return slopes_f[pl.ds(h, 8, stride=32), :] if 0 <= h < 32 else zero8

    for p in range(NC):
        block = [own_row(2 * p - 1 + j) for j in range(4)]
        rows_send[p] = jnp.concatenate(block, axis=0).astype(BF16)
    rows_recv[c] = rows_send[c]
    act_taps[0:32, 128:256] = jnp.zeros((32, 128), BF16)
    act_taps[64:96, 4096:4224] = jnp.zeros((32, 128), BF16)
    act_taps[96:128, :] = jnp.zeros((32, 34 * 128), BF16)
    source = lax.broadcasted_iota(jnp.int32, (256, 256), 0)
    target = lax.broadcasted_iota(jnp.int32, (256, 256), 1)
    slot = (target & 3) * 8 + ((target & 63) >> 3) + ((target >> 6) * 32) + ((target >> 2) & 1) * 128
    spread[...] = jnp.where(source == slot, 1.0, 0.0).astype(BF16)

    loads[1].wait()
    pl.semaphore_wait(barrier, len(greeted))

    for k in (4, 3, 5, 2, 6, 1, 7):
        send(act_all.at[y], act_all.at[y], 0, (d, lax.rem(c + 2 * k, NC)))
    own = slopes_all.at[2 + x]
    send(own, slopes_all.at[4 + x], 1, (up, other))
    send(own, slopes_all.at[x], 1, (down, other))
    send(own, slopes_all.at[2 + x], 1, (d, other))
    send(own, slopes_all.at[4 + x], 1, (up, c))
    send(own, slopes_all.at[x], 1, (down, c))
    for peer in chan_peers:
        send(rows_send.at[peer[1]], rows_recv.at[c], 2, peer)

    drained(slopes_all.at[pl.ds(0, 5)], recv_sem.at[1])
    has_up = jnp.where(d == ND - 1, 0.0, 1.0).astype(F32)
    has_down = jnp.where(d == 0, 0.0, 1.0).astype(F32)
    for a in range(3):
        for xx in range(2):
            value = slopes_all[2 * a + xx].astype(F32)
            if a == 0:
                value = value * has_up
            if a == 2:
                value = value * has_down
            slopes_f[(2 * a + xx) * 256:(2 * a + xx + 1) * 256] = value

    def slope_rows(step, carry):
        for part in range(4):
            h = step * 4 + part
            at = pl.ds(pl.multiple_of(h * 128, 128), 128)
            for a in range(3):
                row = jnp.concatenate(
                    [slopes_f[pl.ds((2 * a + xx) * 256 + h, 8, stride=32), :] for xx in range(2)], axis=0
                )
                left = jnp.where(lane == 127, 0.0, pltpu.roll(row, 127, 1))
                right = jnp.where(lane == 0, 0.0, pltpu.roll(row, 1, 1))
                for third, value in enumerate((left, row, right)):
                    at_row = (3 * a + third) * 16
                    taps[at_row:at_row + 16, at] = value.astype(BF16)
        return carry

    lax.fori_loop(0, 8, slope_rows, 0)

    drained(act_all.at[pl.ds(0, 7)], recv_sem.at[0])
    for p in range(8):
        act_f[p * 128:(p + 1) * 128] = act_all[p].astype(F32)

    def act_rows(step, carry):
        for part in range(4):
            h = step * 4 + part
            row = jnp.concatenate(
                [act_f[pl.ds(i * 32 + h, 8, stride=128), :] for i in range(4)], axis=0
            ).astype(BF16)
            for b in range(3):
                at = pl.ds(pl.multiple_of((h + 2 - b) * 128, 128), 128)
                act_taps[b * 32:(b + 1) * 32, at] = row
        return carry

    lax.fori_loop(0, 8, act_rows, 0)
    terms = lax.dot_general(
        taps[...], act_taps[:, 128:4224], (((1,), (1,)), ((), ())), preferred_element_type=F32
    )

    lane8 = lax.broadcasted_iota(jnp.int32, (8, 128), 1)
    for xx in range(2):
        def tile(a, third):
            at_row = (3 * a + third) * 16 + xx * 8
            return terms[at_row:at_row + 8]
        packed = []
        for a in range(3):
            last = tile(a, 2)
            packed.append(jnp.where(lane8 < 96, tile(a, 0), pltpu.roll(last, 96, 1)))
            packed.append(jnp.where(lane8 < 96, tile(a, 1), pltpu.roll(last, 64, 1)))
        rest = jnp.zeros((8, 128), F32)
        for a in range(3):
            part = pltpu.roll(tile(a, 2), (32 * a - 64) % 128, 1)
            rest = jnp.where((lane8 >= 32 * a) & (lane8 < 32 * a + 32), part, rest)
        packed.append(rest)
        for t in range(7):
            for j in range(4):
                piece_send[xx * 28 + t * 4 + j] = packed[t][2 * j:2 * j + 2]

    for peer in depth_peers:
        @pl.when(owns(peer[0]))
        def _():
            send(piece_send.at[owned(peer[0])], piece_recv.at[d], 3, peer)

    @pl.when(owns(d))
    def _():
        piece_recv[d] = piece_send[owned(d)]

    loads[2].wait()
    drained(rows_recv.at[pl.ds(0, 15)], recv_sem.at[2])
    lane128 = lax.broadcasted_iota(jnp.int32, (128, 128), 1)
    for j in range(4):
        row = rows_recv[:, j * 8:(j + 1) * 8, :].astype(F32).reshape(128, 128)
        left = jnp.where(lane128 == 127, 0.0, pltpu.roll(row, 127, 1))
        right = jnp.where(lane128 == 0, 0.0, pltpu.roll(row, 1, 1))
        for third, value in enumerate((left, row, right)):
            rows_taps[third * 128:(third + 1) * 128, j * 128:(j + 1) * 128] = value.astype(BF16)
    right_side = jnp.concatenate(
        [rows_taps[:, (2 - b) * 128:(4 - b) * 128] for b in range(3)], axis=0
    )

    def plane_term(a):
        left_side = jnp.concatenate(
            [weight_v[(9 * a + k) * 64:(9 * a + k + 1) * 64] for k in range(9)], axis=1
        )
        return jnp.dot(left_side, right_side, preferred_element_type=F32)

    near_send[0] = plane_term(0)
    send(near_send.at[0], near_recv.at[0], 4, (down, c))
    near_send[1] = plane_term(2)
    send(near_send.at[1], near_recv.at[1], 4, (up, c))
    middle = plane_term(1)
    drained(near_recv, recv_sem.at[4])
    whole = middle + near_recv[0] * has_up + near_recv[1] * has_down
    for p in range(NC):
        back_send[p * 8:(p + 1) * 8] = jnp.concatenate(
            [whole[4 * p:4 * p + 4, 0:128], whole[4 * p:4 * p + 4, 128:256]], axis=0
        )
    mine = pl.ds(pl.multiple_of(c * 8, 8), 8)
    back_recv[mine] = back_send[mine]
    for peer in chan_peers:
        theirs = pl.ds(pl.multiple_of(peer[1] * 8, 8), 8)
        send(back_send.at[theirs], back_recv.at[mine], 5, peer)

    @pl.when(owns(d))
    def _():
        drained(piece_recv.at[pl.ds(0, 63)], recv_sem.at[3])
        piece_sum[...] = jnp.sum(piece_recv[...], axis=0)
        q = owned(d)
        to = q // 28
        slot_at = lax.rem(q, 28)
        goal = c - x + to
        for peer in depth_peers:
            send(piece_sum, gathered.at[x, slot_at], 6, (peer[0], goal))

        @pl.when(to == x)
        def _():
            gathered[x, slot_at] = piece_sum[...]

        @pl.when(to != x)
        def _():
            send(piece_sum, gathered.at[x, slot_at], 6, (d, goal))

    drained(back_recv.at[pl.ds(0, 120)], recv_sem.at[5])
    for i in range(4):
        grad_out[i] = back_recv[pl.ds(i, 32, stride=4), :].astype(BF16)

    kept = jnp.logical_and(owns(d), owned(d) // 28 == x)

    @pl.when(kept)
    def _():
        drained(piece_send.at[pl.ds(0, 55)], recv_sem.at[6])

    @pl.when(jnp.logical_not(kept))
    def _():
        drained(piece_send, recv_sem.at[6])

    sides = [gathered[xx].reshape(56, 128) for xx in range(2)]
    both = jnp.concatenate(sides, axis=1)
    high = both.astype(BF16)
    rest = both - high.astype(F32)
    mid = rest.astype(BF16)
    low = (rest - mid.astype(F32)).astype(BF16)
    split = jnp.concatenate([high.astype(F32), mid.astype(F32), low.astype(F32)], axis=0).astype(BF16)
    placed = jnp.dot(split, spread[...], preferred_element_type=F32)
    result = ((placed[0:56] + placed[56:112]) + placed[112:168]) * (1.0 / math.sqrt(ND * 32 * 128))
    for a in range(3):
        for b in range(3):
            for third in range(3):
                if third < 2:
                    t, part = 2 * a + third, b
                elif b < 2:
                    t, part = 2 * a + b, 3
                else:
                    t, part = 6, a
                filt_out[9 * a + 3 * b + third] = result[t * 8:t * 8 + 8, part * 64:part * 64 + 64]

    drained(act_all.at[pl.ds(0, 7)], send_sem.at[0])
    drained(slopes_all.at[pl.ds(0, 5)], send_sem.at[1])
    drained(rows_recv.at[pl.ds(0, 15)], send_sem.at[2])
    drained(near_send, send_sem.at[4])
    drained(back_send.at[pl.ds(0, 120)], send_sem.at[5])

    @pl.when(owns(d))
    def _():
        drained(piece_send.at[pl.ds(0, 55)], send_sem.at[3])

        @pl.when(owned(d) // 28 == x)
        def _():
            drained(piece_recv.at[pl.ds(0, 63)], send_sem.at[6])

        @pl.when(owned(d) // 28 != x)
        def _():
            drained(piece_recv, send_sem.at[6])

    @pl.when(jnp.logical_not(owns(d)))
    def _():
        drained(piece_send, send_sem.at[3])


def per_device(activations, slopes, weight):
    anywhere = pl.BlockSpec(memory_space=pl.ANY)
    vmem = pl.BlockSpec(memory_space=pltpu.VMEM)
    grad, filt = pl.pallas_call(
        kernel,
        name="conv_grads",
        out_shape=(
            jax.ShapeDtypeStruct((4, 32, 128), BF16),
            jax.ShapeDtypeStruct((27, 8, 64), F32),
        ),
        in_specs=[anywhere] * 3,
        out_specs=(vmem, vmem),
        scratch_shapes=[
            pltpu.VMEM((8, 128, 128), BF16),
            pltpu.VMEM((6, 256, 128), BF16),
            pltpu.VMEM((27 * 64, 128), BF16),
            pltpu.VMEM((6 * 256, 128), F32),
            pltpu.VMEM((8 * 128, 128), F32),
            pltpu.VMEM((144, 32 * 128), BF16),
            pltpu.VMEM((128, 34 * 128), BF16),
            pltpu.VMEM((NC, 32, 128), BF16),
            pltpu.VMEM((NC, 32, 128), BF16),
            pltpu.VMEM((384, 512), BF16),
            pltpu.VMEM((2, 64, 256), F32),
            pltpu.VMEM((2, 64, 256), F32),
            pltpu.VMEM((128, 128), F32),
            pltpu.VMEM((128, 128), F32),
            pltpu.VMEM((PIECES, 2, 128), F32),
            pltpu.VMEM((ND, 2, 128), F32),
            pltpu.VMEM((2, 128), F32),
            pltpu.VMEM((2, 28, 2, 128), F32),
            pltpu.VMEM((256, 256), BF16),
            pltpu.SemaphoreType.DMA((3,)),
            pltpu.SemaphoreType.DMA((7,)),
            pltpu.SemaphoreType.DMA((7,)),
        ],
        compiler_params=pltpu.CompilerParams(
            collective_id=0, has_side_effects=True, vmem_limit_bytes=32 * 1024 * 1024
        ),
    )(
        activations.reshape(128, 128),
        slopes.reshape(256, 128),
        weight.reshape(27 * 64, 128),
    )
    return grad.reshape(4, 1, 32, 128), jnp.transpose(filt, (0, 2, 1))


def solution(mesh):
    placed = (P("chan", "depth", None, None), P("chan", "depth", None, None), P())
    return jax.shard_map(
        per_device,
        mesh=mesh,
        in_specs=placed,
        out_specs=(P("chan", "depth", None, None), P(None, None, "chan")),
        check_vma=False,
    )
```

```python
import math

import jax
import jax.numpy as jnp
from jax import lax
from jax.experimental import pallas as pl
from jax.experimental.pallas import tpu as pltpu
from jax.sharding import PartitionSpec as P

MESH = pl.DeviceIdType.MESH
F32, BF16 = jnp.float32, jnp.bfloat16
ND, NC = 64, 16
NZ = 16
NX = 2
LATE = 8
HAND_ON = ((1, ()), (2, ()), (3, ()), (4, (5, 6, 7, 8)), (15, (14, 13, 12, 11, 10, 9)))
CHAN_OFFSETS = (8, 9, 6, 10, 7, 11, 4, 12, 5, 13, 2, 14, 3, 15, 1)


def drained(ref, sem):
    pltpu.make_async_copy(ref, ref, sem).wait()


def kernel(
    act_in, slopes_in, weight_in,
    grad_out, filt_out,
    act_all, seam_act, terms, slopes_all, weight_v, slopes_f, act_f, taps, act_taps,
    rows_send, rows_recv, seam_send, seam_recv, rows_taps, near_send, near_recv, whole_sum, back_send, back_recv,
    quad_send, quad_recv, quarter, piece_recv, piece_sum, gathered, spread,
    local_sem, send_sem, recv_sem,
):
    d, c = lax.axis_index("depth"), lax.axis_index("chan")
    y, x = c // 2, lax.rem(c, 2)
    up, down = lax.rem(d + 1, ND), lax.rem(d + ND - 1, ND)
    other = c ^ 1

    loads = [
        pltpu.make_async_copy(slopes_in, slopes_all.at[2 + x], local_sem.at[0]),
        pltpu.make_async_copy(act_in, act_all.at[y], local_sem.at[1]),
        pltpu.make_async_copy(weight_in, weight_v, local_sem.at[2]),
    ]
    for load in loads:
        load.start()

    half_x, z, core = d // 32, lax.rem(d // 2, NZ), lax.rem(d, 2)
    chan_peers = [(d, lax.rem(c + k, NC)) for k in CHAN_OFFSETS]
    near = [(up, c), (down, c), (up, other), (down, other)]
    owner = z == 0
    barrier = pltpu.get_barrier_semaphore()

    def greet(peer):
        pl.semaphore_signal(barrier, inc=1, device_id=peer, device_id_type=MESH)

    def beside(k):
        return d, lax.rem(c + 2 * k + NC, NC)

    close = [beside(k) for k in (-2, 2, -1, 1)] + [(d, other), (d ^ 32, c), (d ^ 33, c), (down, c), (down, other)]
    seam = jnp.logical_and(owner, core == 0)
    tail = jnp.logical_and(z == NZ - 1, core == 1)
    for peer in close:
        greet(peer)

    @pl.when(jnp.logical_not(tail))
    def _():
        greet((up, c))
        greet((up, other))

    @pl.when(seam)
    def _():
        for k in range(1, 8):
            greet((down, lax.rem(c + 2 * k, NC)))

    @pl.when(owner)
    def _():
        for level in range(1, NZ):
            greet((half_x * 32 + level * 2 + core, c))

    def send(src, dst, group, peer):
        pltpu.make_async_remote_copy(
            src_ref=src, dst_ref=dst, send_sem=send_sem.at[group],
            recv_sem=recv_sem.at[group], device_id=peer, device_id_type=MESH,
        ).start()

    lane = lax.broadcasted_iota(jnp.int32, (16, 128), 1)

    loads[0].wait()
    loads[1].wait()

    @pl.when(seam)
    def _():
        pl.semaphore_wait(barrier, 9)

    @pl.when(jnp.logical_and(owner, core == 1))
    def _():
        pl.semaphore_wait(barrier, 11)

    @pl.when(tail)
    def _():
        pl.semaphore_wait(barrier, 19)

    @pl.when(jnp.logical_not(jnp.logical_or(owner, tail)))
    def _():
        pl.semaphore_wait(barrier, 12)

    def block(k):
        return lax.rem(y + k + 8, 8)

    for group, k in ((0, 2), (1, -2), (2, 1), (2, -1)):
        send(act_all.at[y], act_all.at[y], group, beside(k))
    own = slopes_all.at[2 + x]
    send(own, slopes_all.at[4 + x], 12, (up, other))
    send(own, slopes_all.at[2 + x], 3, (d, other))
    send(own, slopes_all.at[4 + x], 12, (up, c))

    @pl.when(jnp.logical_not(seam))
    def _():
        send(own, slopes_all.at[x], 3, (down, other))
        send(own, slopes_all.at[x], 3, (down, c))

    @pl.when(tail)
    def _():
        for k in (4, 3, 5, 2, 6, 1, 7, 0):
            send(act_all.at[y], seam_act.at[y], 16, (up, lax.rem(c + 2 * k, NC)))

    act_taps[0:32, 128:256] = jnp.zeros((32, 128), BF16)
    act_taps[64:96, 4096:4224] = jnp.zeros((32, 128), BF16)
    act_taps[96:128, :] = jnp.zeros((32, 34 * 128), BF16)
    source = lax.broadcasted_iota(jnp.int32, (256, 256), 0)
    target = lax.broadcasted_iota(jnp.int32, (256, 256), 1)
    slot = (target & 3) * 8 + ((target & 63) >> 3) + ((target >> 6) * 32) + ((target >> 2) & 1) * 128
    spread[...] = jnp.where(source == slot, 1.0, 0.0).astype(BF16)

    def convert(k):
        at = block(k)
        act_f[pl.ds(pl.multiple_of(at * 128, 128), 128)] = act_all[at].astype(F32)

    for group, k in ((0, 2), (1, -2)):
        drained(act_all.at[0], recv_sem.at[group])
        behind = block(-k)
        part = pl.ds(0 if k > 0 else 64, 64)
        send(act_all.at[behind, part], act_all.at[behind, part], 4, beside(k))
        send(act_all.at[behind], act_all.at[behind], 4, beside(k // 2))
    for k in (0, 2, -2):
        convert(k)

    @pl.when(tail)
    def _():
        drained(slopes_all.at[0], recv_sem.at[3])

    @pl.when(jnp.logical_not(tail))
    def _():
        drained(slopes_all.at[pl.ds(0, 3)], recv_sem.at[3])

    drained(slopes_all.at[pl.ds(0, 2)], recv_sem.at[12])
    has_up = jnp.where(d == ND - 1, 0.0, 1.0).astype(F32)
    has_down = jnp.where(d == 0, 0.0, 1.0).astype(F32)
    for a in range(3):
        for xx in range(2):
            value = slopes_all[2 * a + xx].astype(F32)
            if a == 0:
                value = jnp.where(tail, 0.0, value)
            if a == 2:
                value = value * has_down
            slopes_f[(2 * a + xx) * 256:(2 * a + xx + 1) * 256] = value

    def slope_rows(step, carry):
        for part in range(4):
            h = step * 4 + part
            at = pl.ds(pl.multiple_of(h * 128, 128), 128)
            for a in range(3):
                row = jnp.concatenate(
                    [slopes_f[pl.ds((2 * a + xx) * 256 + h, 8, stride=32), :] for xx in range(2)], axis=0
                )
                left = jnp.where(lane == 127, 0.0, pltpu.roll(row, 127, 1))
                right = jnp.where(lane == 0, 0.0, pltpu.roll(row, 1, 1))
                for third, value in enumerate((left, row, right)):
                    at_row = (3 * a + third) * 16
                    taps[at_row:at_row + 16, at] = value.astype(BF16)
        return carry

    lax.fori_loop(0, 8, slope_rows, 0)

    zero8 = jnp.zeros((8, 128), F32)

    def fill_rows(blocks, plane):
        def row(h):
            return slopes_f[pl.ds(plane * 256 + h, 8, stride=32), :] if 0 <= h < 32 else zero8

        for p in range(NC):
            block = [row(2 * p - 1 + j) for j in range(4)]
            blocks[p] = jnp.concatenate(block, axis=0).astype(BF16)

    fill_rows(rows_send, 2 + x)
    rows_recv[c] = rows_send[c]

    drained(act_all.at[pl.ds(0, 2)], recv_sem.at[2])
    convert(1)
    convert(-1)
    drained(act_all.at[pl.ds(0, 3)], recv_sem.at[4])
    for peer in chan_peers:
        send(rows_send.at[peer[1]], rows_recv.at[c], 5, peer)

    @pl.when(seam)
    def _():
        fill_rows(seam_send, 4 + x)
        seam_recv[c] = seam_send[c]
        for peer in chan_peers:
            send(seam_send.at[peer[1]], seam_recv.at[c], 15, peer)

    for k in (3, -3, 4):
        convert(k)

    def act_rows(step, carry):
        for part in range(4):
            h = step * 4 + part
            row = jnp.concatenate(
                [act_f[pl.ds(i * 32 + h, 8, stride=128), :] for i in range(4)], axis=0
            ).astype(BF16)
            for b in range(3):
                at = pl.ds(pl.multiple_of((h + 2 - b) * 128, 128), 128)
                act_taps[b * 32:(b + 1) * 32, at] = row
        return carry

    lax.fori_loop(0, 8, act_rows, 0)

    def filter_terms(rows):
        return lax.dot_general(
            rows, act_taps[:, 128:4224], (((1,), (1,)), ((), ())), preferred_element_type=F32
        )

    terms[...] = filter_terms(taps[...])

    @pl.when(seam)
    def _():
        drained(seam_act, recv_sem.at[16])
        for p in range(8):
            act_f[p * 128:(p + 1) * 128] = seam_act[p].astype(F32)
        lax.fori_loop(0, 8, act_rows, 0)
        terms[0:48] = terms[0:48] + filter_terms(taps[48:96]) * has_down

    lane8 = lax.broadcasted_iota(jnp.int32, (8, 128), 1)
    for xx in range(2):
        def tile(a, third):
            at_row = (3 * a + third) * 16 + xx * 8
            return terms[at_row:at_row + 8]
        packed = []
        for a in range(3):
            last = tile(a, 2)
            packed.append(jnp.where(lane8 < 96, tile(a, 0), pltpu.roll(last, 96, 1)))
            packed.append(jnp.where(lane8 < 96, tile(a, 1), pltpu.roll(last, 64, 1)))
        rest = jnp.zeros((8, 128), F32)
        for a in range(3):
            part = pltpu.roll(tile(a, 2), (32 * a - 64) % 128, 1)
            rest = jnp.where((lane8 >= 32 * a) & (lane8 < 32 * a + 32), part, rest)
        packed.append(rest)
        packed.append(jnp.zeros((8, 128), F32))
        for t in range(8):
            quad_send[t // 4, xx, t % 4] = packed[t]

    place = 2 * half_x + core
    for hop, k in ((1, 1), (1, 0), (0, 1)):
        to_x, to_core = half_x ^ hop, core ^ k
        send(quad_send.at[to_x, to_core], quad_recv.at[place], 6, (d ^ (32 * hop + k), c))
    quad_recv[place] = quad_send[half_x, core]

    @pl.when(jnp.logical_not(owner))
    def _():
        drained(quad_recv.at[pl.ds(0, 3)], recv_sem.at[6])
        quarter[...] = (quad_recv[0] + quad_recv[1]) + (quad_recv[2] + quad_recv[3])

    @pl.when(jnp.logical_and(z > 0, z < LATE))
    def _():
        send(quarter, piece_recv.at[z], 7, (half_x * 32 + core, c))

    @pl.when(z >= LATE)
    def _():
        send(quarter, piece_recv.at[z], 8, (half_x * 32 + core, c))

    loads[2].wait()
    drained(rows_recv.at[pl.ds(0, 15)], recv_sem.at[5])
    lane128 = lax.broadcasted_iota(jnp.int32, (128, 128), 1)

    def column_taps(blocks):
        for j in range(4):
            row = blocks[:, j * 8:(j + 1) * 8, :].astype(F32).reshape(128, 128)
            left = jnp.where(lane128 == 127, 0.0, pltpu.roll(row, 127, 1))
            right = jnp.where(lane128 == 0, 0.0, pltpu.roll(row, 1, 1))
            for third, value in enumerate((left, row, right)):
                rows_taps[third * 128:(third + 1) * 128, j * 128:(j + 1) * 128] = value.astype(BF16)

    def plane_term(a):
        left_side = jnp.concatenate(
            [weight_v[(9 * a + k) * 64:(9 * a + k + 1) * 64] for k in range(9)], axis=1
        )
        right_side = jnp.concatenate(
            [rows_taps[:, (2 - b) * 128:(4 - b) * 128] for b in range(3)], axis=0
        )
        return jnp.dot(left_side, right_side, preferred_element_type=F32)

    column_taps(rows_recv)
    near_send[0] = plane_term(0)
    send(near_send.at[0], near_recv.at[0], 9, (down, c))
    near_send[1] = plane_term(2)

    @pl.when(jnp.logical_not(tail))
    def _():
        send(near_send.at[1], near_recv.at[1], 14, (up, c))

    whole_sum[...] = plane_term(1)

    @pl.when(seam)
    def _():
        drained(seam_recv.at[pl.ds(0, 15)], recv_sem.at[15])
        column_taps(seam_recv)
        near_recv[1] = plane_term(2)

    @pl.when(jnp.logical_not(seam))
    def _():
        drained(near_recv.at[1], recv_sem.at[14])

    drained(near_recv.at[0], recv_sem.at[9])
    whole = whole_sum[...] + near_recv[0] * has_up + near_recv[1] * has_down
    for p in range(NC):
        back_send[p * 8:(p + 1) * 8] = jnp.concatenate(
            [whole[4 * p:4 * p + 4, 0:128], whole[4 * p:4 * p + 4, 128:256]], axis=0
        )
    mine = pl.ds(pl.multiple_of(c * 8, 8), 8)
    back_recv[mine] = back_send[mine]
    for peer in chan_peers:
        theirs = pl.ds(pl.multiple_of(peer[1] * 8, 8), 8)
        send(back_send.at[theirs], back_recv.at[mine], 10, peer)

    goal = c - x + core

    @pl.when(owner)
    def _():
        drained(quad_recv.at[pl.ds(0, 3)], recv_sem.at[6])
        total = (quad_recv[0] + quad_recv[1]) + (quad_recv[2] + quad_recv[3])
        drained(piece_recv.at[pl.ds(0, LATE - 1)], recv_sem.at[7])
        for k in range(1, LATE):
            total = total + piece_recv[k]
        drained(piece_recv.at[pl.ds(0, NZ - LATE)], recv_sem.at[8])
        for k in range(LATE, NZ):
            total = total + piece_recv[k]
        piece_sum[...] = total

        def give(peer):
            send(piece_sum, gathered.at[half_x, x], 11, peer)

        give((d ^ 33, goal))
        give((d ^ 32, goal))
        give((d ^ 1, goal))

        @pl.when(goal == c)
        def _():
            gathered[half_x, x] = total

        @pl.when(goal != c)
        def _():
            give((d, goal))

        for level, _ in HAND_ON:
            for hop in (1, 0):
                give(((half_x ^ hop) * 32 + level * 2 + half_x, goal))

    drained(back_recv.at[pl.ds(0, 120)], recv_sem.at[10])
    for i in range(4):
        grad_out[i] = back_recv[pl.ds(i, 32, stride=4), :].astype(BF16)

    kept = jnp.logical_and(owner, goal == c)

    @pl.when(kept)
    def _():
        drained(piece_recv.at[pl.ds(0, 3)], recv_sem.at[11])

    @pl.when(jnp.logical_and(owner, goal != c))
    def _():
        drained(piece_recv.at[pl.ds(0, 4)], recv_sem.at[11])

    @pl.when(jnp.logical_not(owner))
    def _():
        drained(piece_recv.at[pl.ds(0, 2)], recv_sem.at[11])
        send(gathered.at[core], gathered.at[core], 13, (d ^ 1, c))
        for level, followers in [pair for pair in HAND_ON if pair[1]]:
            @pl.when(z == level)
            def _():
                for follower in followers:
                    send(gathered.at[core], gathered.at[core], 11, (half_x * 32 + follower * 2 + core, c))

        drained(gathered.at[1 - core], recv_sem.at[13])

    sides = [
        jnp.concatenate([gathered[t // 4, xx, t % 4] for t in range(7)], axis=0) for xx in range(2)
    ]
    both = jnp.concatenate(sides, axis=1)
    high = both.astype(BF16)
    rest = both - high.astype(F32)
    mid = rest.astype(BF16)
    low = (rest - mid.astype(F32)).astype(BF16)
    split = jnp.concatenate([high.astype(F32), mid.astype(F32), low.astype(F32)], axis=0).astype(BF16)
    placed = jnp.dot(split, spread[...], preferred_element_type=F32)
    result = ((placed[0:56] + placed[56:112]) + placed[112:168]) * (1.0 / math.sqrt(ND * 32 * 128))
    for a in range(3):
        for b in range(3):
            for third in range(3):
                if third < 2:
                    t, part = 2 * a + third, b
                elif b < 2:
                    t, part = 2 * a + b, 3
                else:
                    t, part = 6, a
                filt_out[9 * a + 3 * b + third] = result[t * 8:t * 8 + 8, part * 64:part * 64 + 64]

    for group in (0, 1):
        drained(act_all.at[0], send_sem.at[group])
    drained(act_all.at[pl.ds(0, 2)], send_sem.at[2])
    drained(slopes_all.at[0], send_sem.at[3])
    drained(slopes_all.at[pl.ds(0, 2)], send_sem.at[12])
    drained(act_all.at[pl.ds(0, 3)], send_sem.at[4])
    drained(rows_recv.at[pl.ds(0, 15)], send_sem.at[5])
    drained(quad_recv.at[pl.ds(0, 3)], send_sem.at[6])
    drained(near_send.at[0], send_sem.at[9])
    drained(back_send.at[pl.ds(0, 120)], send_sem.at[10])

    @pl.when(seam)
    def _():
        drained(seam_recv.at[pl.ds(0, 15)], send_sem.at[15])

    @pl.when(jnp.logical_not(seam))
    def _():
        drained(slopes_all.at[pl.ds(0, 2)], send_sem.at[3])

    @pl.when(tail)
    def _():
        drained(seam_act, send_sem.at[16])

    @pl.when(jnp.logical_not(tail))
    def _():
        drained(near_send.at[1], send_sem.at[14])

    @pl.when(jnp.logical_and(z > 0, z < LATE))
    def _():
        drained(quarter, send_sem.at[7])

    @pl.when(z >= LATE)
    def _():
        drained(quarter, send_sem.at[8])

    @pl.when(owner)
    def _():
        drained(piece_recv.at[pl.ds(0, 3 + 2 * len(HAND_ON))], send_sem.at[11])

    @pl.when(jnp.logical_and(owner, goal != c))
    def _():
        drained(piece_recv.at[0], send_sem.at[11])

    @pl.when(jnp.logical_not(owner))
    def _():
        drained(gathered.at[0], send_sem.at[13])

    for level, followers in [pair for pair in HAND_ON if pair[1]]:
        @pl.when(z == level)
        def _():
            drained(piece_recv.at[pl.ds(0, 2 * len(followers))], send_sem.at[11])


def per_device(activations, slopes, weight):
    hbm = pl.BlockSpec(memory_space=pltpu.HBM)
    vmem = pl.BlockSpec(memory_space=pltpu.VMEM)
    grad, filt = pl.pallas_call(
        kernel,
        name="conv_grads",
        out_shape=(
            jax.ShapeDtypeStruct((4, 32, 128), BF16),
            jax.ShapeDtypeStruct((27, 8, 64), F32),
        ),
        in_specs=[hbm] * 3,
        out_specs=(vmem, vmem),
        scratch_shapes=[
            pltpu.VMEM((8, 128, 128), BF16),
            pltpu.VMEM((8, 128, 128), BF16),
            pltpu.VMEM((144, 128), F32),
            pltpu.VMEM((6, 256, 128), BF16),
            pltpu.VMEM((27 * 64, 128), BF16),
            pltpu.VMEM((6 * 256, 128), F32),
            pltpu.VMEM((8 * 128, 128), F32),
            pltpu.VMEM((144, 32 * 128), BF16),
            pltpu.VMEM((128, 34 * 128), BF16),
            pltpu.VMEM((NC, 32, 128), BF16),
            pltpu.VMEM((NC, 32, 128), BF16),
            pltpu.VMEM((NC, 32, 128), BF16),
            pltpu.VMEM((NC, 32, 128), BF16),
            pltpu.VMEM((384, 512), BF16),
            pltpu.VMEM((2, 64, 256), F32),
            pltpu.VMEM((2, 64, 256), F32),
            pltpu.VMEM((64, 256), F32),
            pltpu.VMEM((128, 128), F32),
            pltpu.VMEM((128, 128), F32),
            pltpu.VMEM((NX, 2, 4, 8, 128), F32),
            pltpu.VMEM((4, 4, 8, 128), F32),
            pltpu.VMEM((4, 8, 128), F32),
            pltpu.VMEM((NZ, 4, 8, 128), F32),
            pltpu.VMEM((4, 8, 128), F32),
            pltpu.VMEM((2, 2, 4, 8, 128), F32),
            pltpu.VMEM((256, 256), BF16),
            pltpu.SemaphoreType.DMA((3,)),
            pltpu.SemaphoreType.DMA((17,)),
            pltpu.SemaphoreType.DMA((17,)),
        ],
        compiler_params=pltpu.CompilerParams(
            collective_id=0, has_side_effects=True, vmem_limit_bytes=32 * 1024 * 1024
        ),
    )(
        pltpu.with_memory_space_constraint(activations.reshape(128, 128), pltpu.HBM),
        pltpu.with_memory_space_constraint(slopes.reshape(256, 128), pltpu.HBM),
        pltpu.with_memory_space_constraint(weight.reshape(27 * 64, 128), pltpu.HBM),
    )
    return grad.reshape(4, 1, 32, 128), jnp.transpose(filt, (0, 2, 1))


def solution(mesh):
    placed = (P("chan", "depth", None, None), P("chan", "depth", None, None), P())
    return jax.shard_map(
        per_device,
        mesh=mesh,
        in_specs=placed,
        out_specs=(P("chan", "depth", None, None), P(None, None, "chan")),
        check_vma=False,
    )
```

```python
import math

import jax
import jax.numpy as jnp
from jax import lax
from jax.experimental import pallas as pl
from jax.experimental.pallas import tpu as pltpu
from jax.sharding import PartitionSpec as P

MESH = pl.DeviceIdType.MESH
F32, BF16 = jnp.float32, jnp.bfloat16
ND, NC = 64, 16
NZ = 16
NX = 2
LATE = 8
HAND_ON = ((1, ()), (2, ()), (3, ()), (4, (5, 6, 7, 8)), (15, (14, 13, 12, 11, 10, 9)))
CHAN_OFFSETS = (8, 9, 6, 10, 7, 11, 4, 12, 5, 13, 2, 14, 3, 15, 1)


def drained(ref, sem):
    pltpu.make_async_copy(ref, ref, sem).wait()


def kernel(
    act_in, slopes_in, weight_in,
    grad_out, filt_out,
    act_all, seam_act, terms, slopes_all, weight_v, slopes_f, act_f, taps, act_taps,
    rows_send, rows_recv, seam_send, seam_recv, rows_taps, near_send, near_recv, whole_sum, back_send, back_recv,
    quad_send, quad_recv, quarter, piece_recv, piece_sum, gathered, spread,
    local_sem, send_sem, recv_sem,
):
    d, c = lax.axis_index("depth"), lax.axis_index("chan")
    y, x = c // 2, lax.rem(c, 2)
    up, down = lax.rem(d + 1, ND), lax.rem(d + ND - 1, ND)
    other = c ^ 1

    loads = [
        pltpu.make_async_copy(slopes_in, slopes_all.at[2 + x], local_sem.at[0]),
        pltpu.make_async_copy(act_in, act_all.at[y], local_sem.at[1]),
        pltpu.make_async_copy(weight_in, weight_v, local_sem.at[2]),
    ]
    half_x, z, core = d // 32, lax.rem(d // 2, NZ), lax.rem(d, 2)
    chan_peers = [(d, lax.rem(c + k, NC)) for k in CHAN_OFFSETS]
    near = [(up, c), (down, c), (up, other), (down, other)]
    owner = z == 0
    barrier = pltpu.get_barrier_semaphore()

    def greet(peer):
        pl.semaphore_signal(barrier, inc=1, device_id=peer, device_id_type=MESH)

    def beside(k):
        return d, lax.rem(c + 2 * k + NC, NC)

    close = [beside(k) for k in (-2, 2, -1, 1)] + [(d, other), (d ^ 32, c), (d ^ 33, c), (down, c), (down, other)]
    seam = jnp.logical_and(owner, core == 0)
    tail = jnp.logical_and(z == NZ - 1, core == 1)
    for peer in close:
        greet(peer)

    @pl.when(jnp.logical_not(tail))
    def _():
        greet((up, c))
        greet((up, other))

    @pl.when(seam)
    def _():
        for k in range(1, 8):
            greet((down, lax.rem(c + 2 * k, NC)))

    @pl.when(owner)
    def _():
        for level in range(1, NZ):
            greet((half_x * 32 + level * 2 + core, c))

    for load in loads:
        load.start()

    def send(src, dst, group, peer):
        pltpu.make_async_remote_copy(
            src_ref=src, dst_ref=dst, send_sem=send_sem.at[group],
            recv_sem=recv_sem.at[group], device_id=peer, device_id_type=MESH,
        ).start()

    loads[0].wait()
    loads[1].wait()

    @pl.when(seam)
    def _():
        pl.semaphore_wait(barrier, 9)

    @pl.when(jnp.logical_and(owner, core == 1))
    def _():
        pl.semaphore_wait(barrier, 11)

    @pl.when(tail)
    def _():
        pl.semaphore_wait(barrier, 19)

    @pl.when(jnp.logical_not(jnp.logical_or(owner, tail)))
    def _():
        pl.semaphore_wait(barrier, 12)

    def block(k):
        return lax.rem(y + k + 8, 8)

    for group, k in ((0, 2), (1, -2), (2, 1), (2, -1)):
        send(act_all.at[y], act_all.at[y], group, beside(k))
    own = slopes_all.at[2 + x]
    send(own, slopes_all.at[2 + x], 18, (d, other))
    send(own, slopes_all.at[4 + x], 20, (up, other))
    send(own, slopes_all.at[4 + x], 12, (up, c))

    @pl.when(jnp.logical_not(seam))
    def _():
        send(own, slopes_all.at[x], 19, (down, other))
        send(own, slopes_all.at[x], 3, (down, c))

    @pl.when(tail)
    def _():
        for k in (4, 3, 5, 2, 6, 1, 7, 0):
            send(act_all.at[y], seam_act.at[y], 16, (up, lax.rem(c + 2 * k, NC)))

    act_taps[0:32, 128:256] = jnp.zeros((32, 128), BF16)
    act_taps[64:96, 4096:4224] = jnp.zeros((32, 128), BF16)
    terms[...] = jnp.zeros((160, 128), F32)
    source = lax.broadcasted_iota(jnp.int32, (256, 256), 0)
    target = lax.broadcasted_iota(jnp.int32, (256, 256), 1)
    slot = (target & 3) * 8 + ((target & 63) >> 3) + ((target >> 6) * 32) + ((target >> 2) & 1) * 128
    spread[...] = jnp.where(source == slot, 1.0, 0.0).astype(BF16)

    def convert(k):
        at = block(k)
        act_f[pl.ds(pl.multiple_of(at * 128, 128), 128)] = act_all[at].astype(F32)

    for group, k in ((0, 2), (1, -2)):
        drained(act_all.at[0], recv_sem.at[group])
        behind = block(-k)
        part = pl.ds(0 if k > 0 else 64, 64)
        send(act_all.at[behind, part], act_all.at[behind, part], 4, beside(k))
        send(act_all.at[behind], act_all.at[behind], 4, beside(k // 2))
    for k in (0, 2, -2):
        convert(k)

    has_up = jnp.where(d == ND - 1, 0.0, 1.0).astype(F32)
    has_down = jnp.where(d == 0, 0.0, 1.0).astype(F32)
    zero8 = jnp.zeros((8, 128), F32)

    def column_slopes(rel, up_group, down_group):
        xx = x if rel == 0 else 1 - x

        @pl.when(jnp.logical_not(tail))
        def _():
            drained(own, recv_sem.at[up_group])

        drained(own, recv_sem.at[down_group])
        if rel == 1:
            drained(own, recv_sem.at[18])
        for a in range(3):
            value = slopes_all[2 * a + xx].astype(F32)
            if a == 0:
                value = jnp.where(tail, 0.0, value)
            if a == 2:
                value = value * has_down
            slopes_f[(2 * a + rel) * 256:(2 * a + rel + 1) * 256] = value

        def slope_rows(step, carry):
            for part in range(4):
                h = step * 4 + part
                at = pl.ds(pl.multiple_of(h * 128, 128), 128)
                shifted = []
                for a in range(3):
                    row = slopes_f[pl.ds((2 * a + rel) * 256 + h, 8, stride=32), :]
                    left = jnp.where(lane8 == 127, 0.0, pltpu.roll(row, 127, 1))
                    right = jnp.where(lane8 == 0, 0.0, pltpu.roll(row, 1, 1))
                    shifted += [left, row, right]
                shifted.append(zero8)
                for t in range(5):
                    at_row = rel * 80 + t * 16
                    both = jnp.concatenate(shifted[2 * t:2 * t + 2], axis=0)
                    taps[at_row:at_row + 16, at] = both.astype(BF16)
            return carry

        lax.fori_loop(0, 8, slope_rows, 0)

    lane8 = lax.broadcasted_iota(jnp.int32, (8, 128), 1)
    column_slopes(0, 3, 12)

    def fill_rows(blocks, plane):
        def row(h):
            return slopes_f[pl.ds(plane * 256 + h, 8, stride=32), :] if 0 <= h < 32 else zero8

        for p in range(NC):
            block = [row(2 * p - 1 + j) for j in range(4)]
            blocks[p] = jnp.concatenate(block, axis=0).astype(BF16)

    fill_rows(rows_send, 2)
    rows_recv[c] = rows_send[c]
    column_slopes(1, 19, 20)

    drained(act_all.at[pl.ds(0, 2)], recv_sem.at[2])
    convert(1)
    convert(-1)
    drained(act_all.at[pl.ds(0, 3)], recv_sem.at[4])
    for peer in chan_peers:
        send(rows_send.at[peer[1]], rows_recv.at[c], 5, peer)

    @pl.when(seam)
    def _():
        fill_rows(seam_send, 4)
        seam_recv[c] = seam_send[c]
        for peer in chan_peers:
            send(seam_send.at[peer[1]], seam_recv.at[c], 15, peer)

    for k in (3, -3, 4):
        convert(k)

    def act_rows(step, carry):
        for part in range(4):
            h = step * 4 + part
            row = jnp.concatenate(
                [act_f[pl.ds(i * 32 + h, 8, stride=128), :] for i in range(4)], axis=0
            ).astype(BF16)
            for b in range(3):
                at = pl.ds(pl.multiple_of((h + 2 - b) * 128, 128), 128)
                act_taps[b * 32:(b + 1) * 32, at] = row
        return carry

    lax.fori_loop(0, 8, act_rows, 0)

    def filter_terms(rows):
        return lax.dot_general(
            rows, act_taps[0:96, 128:4224], (((1,), (1,)), ((), ())), preferred_element_type=F32
        )

    place = 2 * half_x + core

    def pack_and_send(rel):
        def tile(a, third):
            at_row = rel * 80 + (3 * a + third) * 8
            return terms[at_row:at_row + 8]

        packed = []
        for a in range(3):
            last = tile(a, 2)
            packed.append(jnp.where(lane8 < 96, tile(a, 0), pltpu.roll(last, 96, 1)))
            packed.append(jnp.where(lane8 < 96, tile(a, 1), pltpu.roll(last, 64, 1)))
        rest = jnp.zeros((8, 128), F32)
        for a in range(3):
            part = pltpu.roll(tile(a, 2), (32 * a - 64) % 128, 1)
            rest = jnp.where((lane8 >= 32 * a) & (lane8 < 32 * a + 32), part, rest)
        packed.append(rest)
        to_core = 1 - x if rel == 0 else x
        for h in range(NX):
            quad_send[h, to_core, 0:24] = jnp.concatenate(packed[4 * h:4 * h + 3], axis=0)
            quad_send[h, to_core, 24:28] = packed[3][4 * h:4 * h + 4]
        here = d - core + to_core
        send(quad_send.at[1 - half_x, to_core], quad_recv.at[place], 6, (here ^ 32, c))

        @pl.when(to_core != core)
        def _():
            send(quad_send.at[half_x, to_core], quad_recv.at[place], 6, (d ^ 1, c))

    terms[:, 0:96] = filter_terms(taps[...])
    for rel in range(2):
        @pl.when(jnp.logical_not(seam))
        def _():
            pack_and_send(rel)

    @pl.when(seam)
    def _():
        drained(seam_act, recv_sem.at[16])
        for p in range(8):
            act_f[p * 128:(p + 1) * 128] = seam_act[p].astype(F32)
        lax.fori_loop(0, 8, act_rows, 0)
        for rel in range(2):
            at_row = rel * 80
            extra = filter_terms(taps[at_row + 16:at_row + 48])[8:32]
            terms[at_row:at_row + 24, 0:96] = terms[at_row:at_row + 24, 0:96] + extra * has_down
            pack_and_send(rel)

    quad_recv[place] = quad_send[half_x, core]

    @pl.when(jnp.logical_not(owner))
    def _():
        drained(quad_recv.at[pl.ds(0, 3)], recv_sem.at[6])
        quarter[...] = (quad_recv[0] + quad_recv[1]) + (quad_recv[2] + quad_recv[3])

    @pl.when(jnp.logical_and(z > 0, z < LATE))
    def _():
        send(quarter, piece_recv.at[z], 7, (half_x * 32 + core, c))

    @pl.when(z >= LATE)
    def _():
        send(quarter, piece_recv.at[z], 8, (half_x * 32 + core, c))

    loads[2].wait()
    drained(rows_recv.at[pl.ds(0, 15)], recv_sem.at[5])
    lane128 = lax.broadcasted_iota(jnp.int32, (128, 128), 1)

    def column_taps(blocks):
        for j in range(4):
            row = blocks[:, j * 8:(j + 1) * 8, :].astype(F32).reshape(128, 128)
            left = jnp.where(lane128 == 127, 0.0, pltpu.roll(row, 127, 1))
            right = jnp.where(lane128 == 0, 0.0, pltpu.roll(row, 1, 1))
            for third, value in enumerate((left, row, right)):
                rows_taps[third * 128:(third + 1) * 128, j * 128:(j + 1) * 128] = value.astype(BF16)

    def plane_term(a):
        left_side = jnp.concatenate(
            [weight_v[(9 * a + k) * 64:(9 * a + k + 1) * 64] for k in range(9)], axis=1
        )
        right_side = jnp.concatenate(
            [rows_taps[:, (2 - b) * 128:(4 - b) * 128] for b in range(3)], axis=0
        )
        return jnp.dot(left_side, right_side, preferred_element_type=F32)

    column_taps(rows_recv)
    near_send[0] = plane_term(0)
    send(near_send.at[0], near_recv.at[0], 9, (down, c))
    near_send[1] = plane_term(2)

    @pl.when(jnp.logical_not(tail))
    def _():
        send(near_send.at[1], near_recv.at[1], 14, (up, c))

    whole_sum[...] = plane_term(1)

    @pl.when(seam)
    def _():
        drained(seam_recv.at[pl.ds(0, 15)], recv_sem.at[15])
        column_taps(seam_recv)
        near_recv[1] = plane_term(2)

    @pl.when(jnp.logical_not(seam))
    def _():
        drained(near_recv.at[1], recv_sem.at[14])

    drained(near_recv.at[0], recv_sem.at[9])
    whole = whole_sum[...] + near_recv[0] * has_up + near_recv[1] * has_down
    for p in range(NC):
        back_send[p * 8:(p + 1) * 8] = jnp.concatenate(
            [whole[4 * p:4 * p + 4, 0:128], whole[4 * p:4 * p + 4, 128:256]], axis=0
        )
    mine = pl.ds(pl.multiple_of(c * 8, 8), 8)
    back_recv[mine] = back_send[mine]
    for peer in chan_peers:
        theirs = pl.ds(pl.multiple_of(peer[1] * 8, 8), 8)
        send(back_send.at[theirs], back_recv.at[mine], 10, peer)

    goal = c - x + 1 - core

    @pl.when(owner)
    def _():
        drained(quad_recv.at[pl.ds(0, 3)], recv_sem.at[6])
        total = (quad_recv[0] + quad_recv[1]) + (quad_recv[2] + quad_recv[3])
        drained(piece_recv.at[pl.ds(0, LATE - 1)], recv_sem.at[7])
        for k in range(1, LATE):
            total = total + piece_recv[k]
        drained(piece_recv.at[pl.ds(0, NZ - LATE)], recv_sem.at[8])
        for k in range(LATE, NZ):
            total = total + piece_recv[k]
        piece_sum[...] = total

        def give(peer):
            send(piece_sum, gathered.at[half_x, x], 11, peer)

        give((d ^ 33, goal))
        give((d ^ 32, goal))
        give((d ^ 1, goal))

        @pl.when(goal == c)
        def _():
            gathered[half_x, x] = total

        @pl.when(goal != c)
        def _():
            give((d, goal))

        for level, _ in HAND_ON:
            for hop in (1, 0):
                give(((half_x ^ hop) * 32 + level * 2 + half_x, goal))

    drained(back_recv.at[pl.ds(0, 120)], recv_sem.at[10])
    for i in range(4):
        grad_out[i] = back_recv[pl.ds(i, 32, stride=4), :].astype(BF16)

    kept = jnp.logical_and(owner, goal == c)

    @pl.when(kept)
    def _():
        drained(piece_recv.at[pl.ds(0, 3)], recv_sem.at[11])

    @pl.when(jnp.logical_and(owner, goal != c))
    def _():
        drained(piece_recv.at[pl.ds(0, 4)], recv_sem.at[11])

    @pl.when(jnp.logical_not(owner))
    def _():
        drained(piece_recv.at[pl.ds(0, 2)], recv_sem.at[11])
        send(gathered.at[core], gathered.at[core], 13, (d ^ 1, c))
        for level, followers in [pair for pair in HAND_ON if pair[1]]:
            @pl.when(z == level)
            def _():
                for follower in followers:
                    send(gathered.at[core], gathered.at[core], 11, (half_x * 32 + follower * 2 + core, c))

        drained(gathered.at[1 - core], recv_sem.at[13])

    sides = [
        jnp.concatenate(
            [gathered[0, xx, 0:24], gathered[0, xx, 24:28], gathered[1, xx, 24:28], gathered[1, xx, 0:24]], axis=0
        )
        for xx in range(2)
    ]
    both = jnp.concatenate(sides, axis=1)
    high = both.astype(BF16)
    rest = both - high.astype(F32)
    mid = rest.astype(BF16)
    low = (rest - mid.astype(F32)).astype(BF16)
    split = jnp.concatenate([high.astype(F32), mid.astype(F32), low.astype(F32)], axis=0).astype(BF16)
    placed = jnp.dot(split, spread[...], preferred_element_type=F32)
    result = ((placed[0:56] + placed[56:112]) + placed[112:168]) * (1.0 / math.sqrt(ND * 32 * 128))
    for a in range(3):
        for b in range(3):
            for third in range(3):
                if third < 2:
                    t, part = 2 * a + third, b
                elif b < 2:
                    t, part = 2 * a + b, 3
                else:
                    t, part = 6, a
                filt_out[9 * a + 3 * b + third] = result[t * 8:t * 8 + 8, part * 64:part * 64 + 64]

    for group in (0, 1):
        drained(act_all.at[0], send_sem.at[group])
    drained(act_all.at[pl.ds(0, 2)], send_sem.at[2])
    for group in (12, 18, 20):
        drained(own, send_sem.at[group])
    drained(act_all.at[pl.ds(0, 3)], send_sem.at[4])
    drained(rows_recv.at[pl.ds(0, 15)], send_sem.at[5])
    drained(quad_recv.at[pl.ds(0, 3)], send_sem.at[6])
    drained(near_send.at[0], send_sem.at[9])
    drained(back_send.at[pl.ds(0, 120)], send_sem.at[10])

    @pl.when(seam)
    def _():
        drained(seam_recv.at[pl.ds(0, 15)], send_sem.at[15])

    @pl.when(jnp.logical_not(seam))
    def _():
        drained(own, send_sem.at[3])
        drained(own, send_sem.at[19])

    @pl.when(tail)
    def _():
        drained(seam_act, send_sem.at[16])

    @pl.when(jnp.logical_not(tail))
    def _():
        drained(near_send.at[1], send_sem.at[14])

    @pl.when(jnp.logical_and(z > 0, z < LATE))
    def _():
        drained(quarter, send_sem.at[7])

    @pl.when(z >= LATE)
    def _():
        drained(quarter, send_sem.at[8])

    @pl.when(owner)
    def _():
        drained(piece_recv.at[pl.ds(0, 3 + 2 * len(HAND_ON))], send_sem.at[11])

    @pl.when(jnp.logical_and(owner, goal != c))
    def _():
        drained(piece_recv.at[0], send_sem.at[11])

    @pl.when(jnp.logical_not(owner))
    def _():
        drained(gathered.at[0], send_sem.at[13])

    for level, followers in [pair for pair in HAND_ON if pair[1]]:
        @pl.when(z == level)
        def _():
            drained(piece_recv.at[pl.ds(0, 2 * len(followers))], send_sem.at[11])


def write_out(grad_in, filt_in, grad_out, filt_out):
    grad_out[...] = grad_in[...]
    filt_out[...] = filt_in[...]


def per_device(activations, slopes, weight):
    hbm = pl.BlockSpec(memory_space=pltpu.HBM)
    vmem = pl.BlockSpec(memory_space=pltpu.VMEM)
    grad, filt = pl.pallas_call(
        kernel,
        name="conv_grads",
        out_shape=(pltpu.VMEM((4, 32, 128), BF16), pltpu.VMEM((27, 8, 64), F32)),
        in_specs=[hbm] * 3,
        out_specs=(vmem, vmem),
        scratch_shapes=[
            pltpu.VMEM((8, 128, 128), BF16),
            pltpu.VMEM((8, 128, 128), BF16),
            pltpu.VMEM((160, 128), F32),
            pltpu.VMEM((6, 256, 128), BF16),
            pltpu.VMEM((27 * 64, 128), BF16),
            pltpu.VMEM((6 * 256, 128), F32),
            pltpu.VMEM((8 * 128, 128), F32),
            pltpu.VMEM((160, 32 * 128), BF16),
            pltpu.VMEM((96, 34 * 128), BF16),
            pltpu.VMEM((NC, 32, 128), BF16),
            pltpu.VMEM((NC, 32, 128), BF16),
            pltpu.VMEM((NC, 32, 128), BF16),
            pltpu.VMEM((NC, 32, 128), BF16),
            pltpu.VMEM((384, 512), BF16),
            pltpu.VMEM((2, 64, 256), F32),
            pltpu.VMEM((2, 64, 256), F32),
            pltpu.VMEM((64, 256), F32),
            pltpu.VMEM((128, 128), F32),
            pltpu.VMEM((128, 128), F32),
            pltpu.VMEM((NX, 2, 28, 128), F32),
            pltpu.VMEM((4, 28, 128), F32),
            pltpu.VMEM((28, 128), F32),
            pltpu.VMEM((NZ, 28, 128), F32),
            pltpu.VMEM((28, 128), F32),
            pltpu.VMEM((2, 2, 28, 128), F32),
            pltpu.VMEM((256, 256), BF16),
            pltpu.SemaphoreType.DMA((3,)),
            pltpu.SemaphoreType.DMA((21,)),
            pltpu.SemaphoreType.DMA((21,)),
        ],
        compiler_params=pltpu.CompilerParams(
            collective_id=0, has_side_effects=True, vmem_limit_bytes=32 * 1024 * 1024
        ),
    )(
        pltpu.with_memory_space_constraint(activations.reshape(128, 128), pltpu.HBM),
        pltpu.with_memory_space_constraint(slopes.reshape(256, 128), pltpu.HBM),
        pltpu.with_memory_space_constraint(weight.reshape(27 * 64, 128), pltpu.HBM),
    )
    grad, filt = pl.pallas_call(
        write_out,
        name="write_out",
        out_shape=(
            jax.ShapeDtypeStruct((4, 32, 128), BF16),
            jax.ShapeDtypeStruct((27, 8, 64), F32),
        ),
        in_specs=[vmem] * 2,
        out_specs=(vmem, vmem),
    )(pltpu.with_memory_space_constraint(grad, pltpu.VMEM), pltpu.with_memory_space_constraint(filt, pltpu.VMEM))
    return grad.reshape(4, 1, 32, 128), jnp.transpose(filt, (0, 2, 1))


def solution(mesh):
    placed = (P("chan", "depth", None, None), P("chan", "depth", None, None), P())
    return jax.shard_map(
        per_device,
        mesh=mesh,
        in_specs=placed,
        out_specs=(P("chan", "depth", None, None), P(None, None, "chan")),
        check_vma=False,
    )
```

```python
import math

import jax
import jax.numpy as jnp
from jax import lax
from jax.experimental import pallas as pl
from jax.experimental.pallas import tpu as pltpu
from jax.sharding import PartitionSpec as P

MESH = pl.DeviceIdType.MESH
F32, BF16 = jnp.float32, jnp.bfloat16
ND, NC = 64, 16
NZ = 16
NX = 2
LATE = 8
HAND_ON = ((1, ()), (2, ()), (3, ()), (4, (5, 6, 7, 8)), (15, (14, 13, 12, 11, 10, 9)))
CHAN_OFFSETS = (8, 9, 6, 10, 7, 11, 4, 12, 5, 13, 2, 14, 3, 15, 1)


def drained(ref, sem):
    pltpu.make_async_copy(ref, ref, sem).wait()


def kernel(
    act_in, slopes_in, weight_in,
    grad_out, filt_out,
    act_all, seam_act, terms, slopes_all, weight_v, slopes_f, act_f, taps, act_taps,
    rows_send, rows_recv, seam_send, seam_recv, rows_taps, near_send, near_recv, whole_sum, back_send, back_recv,
    quad_send, quad_recv, quarter, piece_recv, piece_sum, gathered, spread,
    local_sem, send_sem, recv_sem,
):
    d, c = lax.axis_index("depth"), lax.axis_index("chan")
    y, x = c // 2, lax.rem(c, 2)
    up, down = lax.rem(d + 1, ND), lax.rem(d + ND - 1, ND)
    other = c ^ 1

    loads = [
        pltpu.make_async_copy(slopes_in, slopes_all.at[2 + x], local_sem.at[0]),
        pltpu.make_async_copy(act_in, act_all.at[y], local_sem.at[1]),
        pltpu.make_async_copy(weight_in, weight_v, local_sem.at[2]),
    ]
    half_x, z, core = d // 32, lax.rem(d // 2, NZ), lax.rem(d, 2)
    chan_peers = [(d, lax.rem(c + k, NC)) for k in CHAN_OFFSETS]
    near = [(up, c), (down, c), (up, other), (down, other)]
    owner = z == 0
    barrier = pltpu.get_barrier_semaphore()

    def greet(peer):
        pl.semaphore_signal(barrier, inc=1, device_id=peer, device_id_type=MESH)

    def beside(k):
        return d, lax.rem(c + 2 * k + NC, NC)

    close = [beside(k) for k in (-2, 2, -1, 1)] + [(d, other), (d ^ 32, c), (d ^ 33, c), (down, c), (down, other)]
    seam = jnp.logical_and(owner, core == 0)
    tail = jnp.logical_and(z == NZ - 1, core == 1)
    for peer in close:
        greet(peer)

    @pl.when(jnp.logical_not(tail))
    def _():
        greet((up, c))
        greet((up, other))

    @pl.when(seam)
    def _():
        for k in range(1, 8):
            greet((down, lax.rem(c + 2 * k, NC)))

    @pl.when(owner)
    def _():
        for level in range(1, NZ):
            greet((half_x * 32 + level * 2 + core, c))

    for load in loads:
        load.start()

    def send(src, dst, group, peer):
        pltpu.make_async_remote_copy(
            src_ref=src, dst_ref=dst, send_sem=send_sem.at[group],
            recv_sem=recv_sem.at[group], device_id=peer, device_id_type=MESH,
        ).start()

    loads[0].wait()
    loads[1].wait()

    @pl.when(seam)
    def _():
        pl.semaphore_wait(barrier, 9)

    @pl.when(jnp.logical_and(owner, core == 1))
    def _():
        pl.semaphore_wait(barrier, 11)

    @pl.when(tail)
    def _():
        pl.semaphore_wait(barrier, 19)

    @pl.when(jnp.logical_not(jnp.logical_or(owner, tail)))
    def _():
        pl.semaphore_wait(barrier, 12)

    def block(k):
        return lax.rem(y + k + 8, 8)

    for group, k in ((0, 2), (1, -2)):
        send(act_all.at[y], act_all.at[y], group, beside(k))
    own = slopes_all.at[2 + x]
    send(own, slopes_all.at[2 + x], 18, (d, other))
    send(own, slopes_all.at[4 + x], 12, (up, c))

    @pl.when(core == 1)
    def _():
        send(own, slopes_all.at[4 + x], 20, (up, other))

    @pl.when(jnp.logical_and(core == 0, jnp.logical_not(seam)))
    def _():
        send(own, slopes_all.at[x], 19, (down, other))

    @pl.when(jnp.logical_not(seam))
    def _():
        send(own, slopes_all.at[x], 3, (down, c))

    @pl.when(tail)
    def _():
        for k in (4, 3, 5, 2, 6, 1, 7, 0):
            send(act_all.at[y], seam_act.at[y], 16, (up, lax.rem(c + 2 * k, NC)))

    act_taps[0:32, 128:256] = jnp.zeros((32, 128), BF16)
    act_taps[64:96, 4096:4224] = jnp.zeros((32, 128), BF16)
    terms[...] = jnp.zeros((160, 128), F32)
    source = lax.broadcasted_iota(jnp.int32, (256, 256), 0)
    target = lax.broadcasted_iota(jnp.int32, (256, 256), 1)
    slot = (target & 3) * 8 + ((target & 63) >> 3) + ((target >> 6) * 32) + ((target >> 2) & 1) * 128
    spread[...] = jnp.where(source == slot, 1.0, 0.0).astype(BF16)

    def convert(k):
        at = block(k)
        act_f[pl.ds(pl.multiple_of(at * 128, 128), 128)] = act_all[at].astype(F32)

    for group, k in ((1, -2), (0, 2)):
        drained(act_all.at[0], recv_sem.at[group])
        behind = block(-k)
        part = pl.ds(0 if k > 0 else 64, 64)
        send(act_all.at[behind, part], act_all.at[behind, part], 4, beside(k))
        send(act_all.at[behind], act_all.at[behind], 4, beside(k // 2))
    for k in (1, -1):
        send(act_all.at[y], act_all.at[y], 2, beside(k))

    drained(own, recv_sem.at[18])
    across = slopes_all.at[3 - x]

    @pl.when(core == 0)
    def _():
        send(across, slopes_all.at[5 - x], 20, (up, c))

    @pl.when(core == 1)
    def _():
        send(across, slopes_all.at[1 - x], 19, (down, c))

    for k in (0, 2, -2):
        convert(k)

    has_up = jnp.where(d == ND - 1, 0.0, 1.0).astype(F32)
    has_down = jnp.where(d == 0, 0.0, 1.0).astype(F32)
    zero8 = jnp.zeros((8, 128), F32)

    def column_slopes(rel, up_group, down_group):
        xx = x if rel == 0 else 1 - x

        @pl.when(jnp.logical_not(tail))
        def _():
            drained(own, recv_sem.at[up_group])

        drained(own, recv_sem.at[down_group])
        for a in range(3):
            value = slopes_all[2 * a + xx].astype(F32)
            if a == 0:
                value = jnp.where(tail, 0.0, value)
            if a == 2:
                value = value * has_down
            slopes_f[(2 * a + rel) * 256:(2 * a + rel + 1) * 256] = value

        def slope_rows(step, carry):
            for part in range(4):
                h = step * 4 + part
                at = pl.ds(pl.multiple_of(h * 128, 128), 128)
                shifted = []
                for a in range(3):
                    row = slopes_f[pl.ds((2 * a + rel) * 256 + h, 8, stride=32), :]
                    left = jnp.where(lane8 == 127, 0.0, pltpu.roll(row, 127, 1))
                    right = jnp.where(lane8 == 0, 0.0, pltpu.roll(row, 1, 1))
                    shifted += [left, row, right]
                shifted.append(zero8)
                for t in range(5):
                    at_row = rel * 80 + t * 16
                    both = jnp.concatenate(shifted[2 * t:2 * t + 2], axis=0)
                    taps[at_row:at_row + 16, at] = both.astype(BF16)
            return carry

        lax.fori_loop(0, 8, slope_rows, 0)

    lane8 = lax.broadcasted_iota(jnp.int32, (8, 128), 1)
    column_slopes(0, 3, 12)

    def fill_rows(blocks, plane):
        def row(h):
            return slopes_f[pl.ds(plane * 256 + h, 8, stride=32), :] if 0 <= h < 32 else zero8

        for p in range(NC):
            block = [row(2 * p - 1 + j) for j in range(4)]
            blocks[p] = jnp.concatenate(block, axis=0).astype(BF16)

    fill_rows(rows_send, 2)
    rows_recv[c] = rows_send[c]
    column_slopes(1, 19, 20)

    drained(act_all.at[pl.ds(0, 2)], recv_sem.at[2])
    convert(1)
    convert(-1)
    drained(act_all.at[pl.ds(0, 3)], recv_sem.at[4])

    def send_rows():
        for peer in chan_peers:
            send(rows_send.at[peer[1]], rows_recv.at[c], 5, peer)

    @pl.when(seam)
    def _():
        send_rows()
        fill_rows(seam_send, 4)
        seam_recv[c] = seam_send[c]
        for peer in chan_peers:
            send(seam_send.at[peer[1]], seam_recv.at[c], 15, peer)

    for k in (3, -3, 4):
        convert(k)

    def act_rows(step, carry):
        for part in range(4):
            h = step * 4 + part
            row = jnp.concatenate(
                [act_f[pl.ds(i * 32 + h, 8, stride=128), :] for i in range(4)], axis=0
            ).astype(BF16)
            for b in range(3):
                at = pl.ds(pl.multiple_of((h + 2 - b) * 128, 128), 128)
                act_taps[b * 32:(b + 1) * 32, at] = row
        return carry

    lax.fori_loop(0, 8, act_rows, 0)

    def filter_terms(rows):
        return lax.dot_general(
            rows, act_taps[0:96, 128:4224], (((1,), (1,)), ((), ())), preferred_element_type=F32
        )

    place = 2 * half_x + core

    def pack_and_send(to_core):
        rel = x if to_core == 1 else 1 - x

        def tile(a, third):
            return terms[pl.ds(pl.multiple_of(rel * 80 + (3 * a + third) * 8, 8), 8)]

        packed = []
        for a in range(3):
            last = tile(a, 2)
            packed.append(jnp.where(lane8 < 96, tile(a, 0), pltpu.roll(last, 96, 1)))
            packed.append(jnp.where(lane8 < 96, tile(a, 1), pltpu.roll(last, 64, 1)))
        rest = jnp.zeros((8, 128), F32)
        for a in range(3):
            part = pltpu.roll(tile(a, 2), (32 * a - 64) % 128, 1)
            rest = jnp.where((lane8 >= 32 * a) & (lane8 < 32 * a + 32), part, rest)
        packed.append(rest)
        for h in range(NX):
            quad_send[h, to_core, 0:24] = jnp.concatenate(packed[4 * h:4 * h + 3], axis=0)
            quad_send[h, to_core, 24:28] = packed[3][4 * h:4 * h + 4]
        here = d - core + to_core
        send(quad_send.at[1 - half_x, to_core], quad_recv.at[place], 6, (here ^ 32, c))

        @pl.when(to_core != core)
        def _():
            send(quad_send.at[half_x, to_core], quad_recv.at[place], 6, (d ^ 1, c))

    terms[:, 0:96] = filter_terms(taps[...])

    @pl.when(d != ND // 2)
    def _():
        for to_core in (1, 0):
            pack_and_send(to_core)

    pl.when(jnp.logical_not(seam))(send_rows)

    @pl.when(d == ND // 2)
    def _():
        drained(seam_act, recv_sem.at[16])
        for p in range(8):
            act_f[p * 128:(p + 1) * 128] = seam_act[p].astype(F32)
        lax.fori_loop(0, 8, act_rows, 0)
        extra = filter_terms(taps[16:128])
        for rel in range(2):
            at_row = rel * 80
            terms[at_row:at_row + 24, 0:96] = terms[at_row:at_row + 24, 0:96] + extra[at_row + 8:at_row + 32]
        for to_core in (1, 0):
            pack_and_send(to_core)

    quad_recv[place] = quad_send[half_x, core]

    @pl.when(jnp.logical_not(owner))
    def _():
        drained(quad_recv.at[pl.ds(0, 3)], recv_sem.at[6])
        quarter[...] = (quad_recv[0] + quad_recv[1]) + (quad_recv[2] + quad_recv[3])

    @pl.when(jnp.logical_and(z > 0, z < LATE))
    def _():
        send(quarter, piece_recv.at[z], 7, (half_x * 32 + core, c))

    @pl.when(z >= LATE)
    def _():
        send(quarter, piece_recv.at[z], 8, (half_x * 32 + core, c))

    loads[2].wait()
    drained(rows_recv.at[pl.ds(0, 15)], recv_sem.at[5])
    lane128 = lax.broadcasted_iota(jnp.int32, (128, 128), 1)

    def column_taps(blocks):
        for j in range(4):
            row = blocks[:, j * 8:(j + 1) * 8, :].astype(F32).reshape(128, 128)
            left = jnp.where(lane128 == 127, 0.0, pltpu.roll(row, 127, 1))
            right = jnp.where(lane128 == 0, 0.0, pltpu.roll(row, 1, 1))
            for third, value in enumerate((left, row, right)):
                rows_taps[third * 128:(third + 1) * 128, j * 128:(j + 1) * 128] = value.astype(BF16)

    def plane_term(a):
        left_side = jnp.concatenate(
            [weight_v[(9 * a + k) * 64:(9 * a + k + 1) * 64] for k in range(9)], axis=1
        )
        right_side = jnp.concatenate(
            [rows_taps[:, (2 - b) * 128:(4 - b) * 128] for b in range(3)], axis=0
        )
        return jnp.dot(left_side, right_side, preferred_element_type=F32)

    column_taps(rows_recv)
    near_send[0] = plane_term(0)
    send(near_send.at[0], near_recv.at[0], 9, (down, c))
    near_send[1] = plane_term(2)

    @pl.when(jnp.logical_not(tail))
    def _():
        send(near_send.at[1], near_recv.at[1], 14, (up, c))

    whole_sum[...] = plane_term(1)

    @pl.when(seam)
    def _():
        drained(seam_recv.at[pl.ds(0, 15)], recv_sem.at[15])
        column_taps(seam_recv)
        near_recv[1] = plane_term(2)

    @pl.when(jnp.logical_not(seam))
    def _():
        drained(near_recv.at[1], recv_sem.at[14])

    drained(near_recv.at[0], recv_sem.at[9])
    whole = whole_sum[...] + near_recv[0] * has_up + near_recv[1] * has_down
    for p in range(NC):
        back_send[p * 8:(p + 1) * 8] = jnp.concatenate(
            [whole[4 * p:4 * p + 4, 0:128], whole[4 * p:4 * p + 4, 128:256]], axis=0
        )
    mine = pl.ds(pl.multiple_of(c * 8, 8), 8)
    back_recv[mine] = back_send[mine]
    for peer in chan_peers:
        theirs = pl.ds(pl.multiple_of(peer[1] * 8, 8), 8)
        send(back_send.at[theirs], back_recv.at[mine], 10, peer)

    goal = c - x + 1 - core

    @pl.when(owner)
    def _():
        drained(quad_recv.at[pl.ds(0, 3)], recv_sem.at[6])
        total = (quad_recv[0] + quad_recv[1]) + (quad_recv[2] + quad_recv[3])
        drained(piece_recv.at[pl.ds(0, LATE - 1)], recv_sem.at[7])
        for k in range(1, LATE):
            total = total + piece_recv[k]
        drained(piece_recv.at[pl.ds(0, NZ - LATE)], recv_sem.at[8])
        for k in range(LATE, NZ):
            total = total + piece_recv[k]
        piece_sum[...] = total

        def give(peer):
            send(piece_sum, gathered.at[half_x, x], 11, peer)

        give((d ^ 32, goal))
        give((d ^ 33, goal))
        give((d ^ 1, goal))

        @pl.when(goal == c)
        def _():
            gathered[half_x, x] = total

        @pl.when(goal != c)
        def _():
            give((d, goal))

        for level, _ in HAND_ON:
            for hop in (1, 0):
                give(((half_x ^ hop) * 32 + level * 2 + half_x, goal))

    drained(back_recv.at[pl.ds(0, 120)], recv_sem.at[10])
    for i in range(4):
        grad_out[i] = back_recv[pl.ds(i, 32, stride=4), :].astype(BF16)

    kept = jnp.logical_and(owner, goal == c)

    @pl.when(kept)
    def _():
        drained(piece_recv.at[pl.ds(0, 3)], recv_sem.at[11])

    @pl.when(jnp.logical_and(owner, goal != c))
    def _():
        drained(piece_recv.at[pl.ds(0, 4)], recv_sem.at[11])

    @pl.when(jnp.logical_not(owner))
    def _():
        drained(piece_recv.at[pl.ds(0, 2)], recv_sem.at[11])
        send(gathered.at[core], gathered.at[core], 13, (d ^ 1, c))
        for level, followers in [pair for pair in HAND_ON if pair[1]]:
            @pl.when(z == level)
            def _():
                for follower in followers:
                    send(gathered.at[core], gathered.at[core], 11, (half_x * 32 + follower * 2 + core, c))

        drained(gathered.at[1 - core], recv_sem.at[13])

    sides = [
        jnp.concatenate(
            [gathered[0, xx, 0:24], gathered[0, xx, 24:28], gathered[1, xx, 24:28], gathered[1, xx, 0:24]], axis=0
        )
        for xx in range(2)
    ]
    both = jnp.concatenate(sides, axis=1)
    high = both.astype(BF16)
    rest = both - high.astype(F32)
    mid = rest.astype(BF16)
    low = (rest - mid.astype(F32)).astype(BF16)
    split = jnp.concatenate([high.astype(F32), mid.astype(F32), low.astype(F32)], axis=0).astype(BF16)
    placed = jnp.dot(split, spread[...], preferred_element_type=F32)
    result = ((placed[0:56] + placed[56:112]) + placed[112:168]) * (1.0 / math.sqrt(ND * 32 * 128))
    for a in range(3):
        for b in range(3):
            for third in range(3):
                if third < 2:
                    t, part = 2 * a + third, b
                elif b < 2:
                    t, part = 2 * a + b, 3
                else:
                    t, part = 6, a
                filt_out[9 * a + 3 * b + third] = result[t * 8:t * 8 + 8, part * 64:part * 64 + 64]

    @pl.when(d == 0)
    def _():
        drained(seam_act, recv_sem.at[16])

    for group in (0, 1):
        drained(act_all.at[0], send_sem.at[group])
    drained(act_all.at[pl.ds(0, 2)], send_sem.at[2])
    for group in (12, 18, 20):
        drained(own, send_sem.at[group])
    drained(act_all.at[pl.ds(0, 3)], send_sem.at[4])
    drained(rows_recv.at[pl.ds(0, 15)], send_sem.at[5])
    drained(quad_recv.at[pl.ds(0, 3)], send_sem.at[6])
    drained(near_send.at[0], send_sem.at[9])
    drained(back_send.at[pl.ds(0, 120)], send_sem.at[10])

    @pl.when(seam)
    def _():
        drained(seam_recv.at[pl.ds(0, 15)], send_sem.at[15])

    @pl.when(jnp.logical_not(seam))
    def _():
        drained(own, send_sem.at[3])
        drained(own, send_sem.at[19])

    @pl.when(tail)
    def _():
        drained(seam_act, send_sem.at[16])

    @pl.when(jnp.logical_not(tail))
    def _():
        drained(near_send.at[1], send_sem.at[14])

    @pl.when(jnp.logical_and(z > 0, z < LATE))
    def _():
        drained(quarter, send_sem.at[7])

    @pl.when(z >= LATE)
    def _():
        drained(quarter, send_sem.at[8])

    @pl.when(owner)
    def _():
        drained(piece_recv.at[pl.ds(0, 3 + 2 * len(HAND_ON))], send_sem.at[11])

    @pl.when(jnp.logical_and(owner, goal != c))
    def _():
        drained(piece_recv.at[0], send_sem.at[11])

    @pl.when(jnp.logical_not(owner))
    def _():
        drained(gathered.at[0], send_sem.at[13])

    for level, followers in [pair for pair in HAND_ON if pair[1]]:
        @pl.when(z == level)
        def _():
            drained(piece_recv.at[pl.ds(0, 2 * len(followers))], send_sem.at[11])


def write_out(grad_in, filt_in, grad_out, filt_out):
    grad_out[...] = grad_in[...]
    filt_out[...] = filt_in[...]


def per_device(activations, slopes, weight):
    hbm = pl.BlockSpec(memory_space=pltpu.HBM)
    vmem = pl.BlockSpec(memory_space=pltpu.VMEM)
    grad, filt = pl.pallas_call(
        kernel,
        name="conv_grads",
        out_shape=(pltpu.VMEM((4, 32, 128), BF16), pltpu.VMEM((27, 8, 64), F32)),
        in_specs=[hbm] * 3,
        out_specs=(vmem, vmem),
        scratch_shapes=[
            pltpu.VMEM((8, 128, 128), BF16),
            pltpu.VMEM((8, 128, 128), BF16),
            pltpu.VMEM((160, 128), F32),
            pltpu.VMEM((6, 256, 128), BF16),
            pltpu.VMEM((27 * 64, 128), BF16),
            pltpu.VMEM((6 * 256, 128), F32),
            pltpu.VMEM((8 * 128, 128), F32),
            pltpu.VMEM((160, 32 * 128), BF16),
            pltpu.VMEM((96, 34 * 128), BF16),
            pltpu.VMEM((NC, 32, 128), BF16),
            pltpu.VMEM((NC, 32, 128), BF16),
            pltpu.VMEM((NC, 32, 128), BF16),
            pltpu.VMEM((NC, 32, 128), BF16),
            pltpu.VMEM((384, 512), BF16),
            pltpu.VMEM((2, 64, 256), F32),
            pltpu.VMEM((2, 64, 256), F32),
            pltpu.VMEM((64, 256), F32),
            pltpu.VMEM((128, 128), F32),
            pltpu.VMEM((128, 128), F32),
            pltpu.VMEM((NX, 2, 28, 128), F32),
            pltpu.VMEM((4, 28, 128), F32),
            pltpu.VMEM((28, 128), F32),
            pltpu.VMEM((NZ, 28, 128), F32),
            pltpu.VMEM((28, 128), F32),
            pltpu.VMEM((2, 2, 28, 128), F32),
            pltpu.VMEM((256, 256), BF16),
            pltpu.SemaphoreType.DMA((3,)),
            pltpu.SemaphoreType.DMA((21,)),
            pltpu.SemaphoreType.DMA((21,)),
        ],
        compiler_params=pltpu.CompilerParams(
            collective_id=0, has_side_effects=True, vmem_limit_bytes=32 * 1024 * 1024
        ),
    )(
        pltpu.with_memory_space_constraint(activations.reshape(128, 128), pltpu.HBM),
        pltpu.with_memory_space_constraint(slopes.reshape(256, 128), pltpu.HBM),
        pltpu.with_memory_space_constraint(weight.reshape(27 * 64, 128), pltpu.HBM),
    )
    grad, filt = pl.pallas_call(
        write_out,
        name="write_out",
        out_shape=(
            jax.ShapeDtypeStruct((4, 32, 128), BF16),
            jax.ShapeDtypeStruct((27, 8, 64), F32),
        ),
        in_specs=[vmem] * 2,
        out_specs=(vmem, vmem),
    )(pltpu.with_memory_space_constraint(grad, pltpu.VMEM), pltpu.with_memory_space_constraint(filt, pltpu.VMEM))
    return grad.reshape(4, 1, 32, 128), jnp.transpose(filt, (0, 2, 1))


def solution(mesh):
    placed = (P("chan", "depth", None, None), P("chan", "depth", None, None), P())
    return jax.shard_map(
        per_device,
        mesh=mesh,
        in_specs=placed,
        out_specs=(P("chan", "depth", None, None), P(None, None, "chan")),
        check_vma=False,
    )
```

```python
import math

import jax
import jax.numpy as jnp
from jax import lax
from jax.experimental import pallas as pl
from jax.experimental.pallas import tpu as pltpu
from jax.sharding import PartitionSpec as P

MESH = pl.DeviceIdType.MESH
F32, BF16 = jnp.float32, jnp.bfloat16
ND, NC = 64, 16
NZ = 16
NX = 2
LATE = 8
HAND_ON = ((1, ()), (2, ()), (3, ()), (4, ()), (5, (6, 7, 8)), (15, (14, 13, 12, 11, 10, 9)))
CHAN_OFFSETS = (8, 9, 6, 10, 7, 11, 4, 12, 5, 13, 2, 14, 3, 15, 1)


def drained(ref, sem):
    pltpu.make_async_copy(ref, ref, sem).wait()


def kernel(
    act_in, slopes_in, weight_in,
    grad_out, filt_out,
    act_all, seam_act, terms, slopes_all, weight_v, slopes_f, act_f, taps, act_taps,
    rows_send, rows_recv, seam_send, seam_recv, rows_taps, near_send, near_recv, whole_sum, back_send, back_recv,
    quad_send, quad_recv, quarter, piece_recv, piece_sum, gathered, spread,
    local_sem, send_sem, recv_sem,
):
    d, c = lax.axis_index("depth"), lax.axis_index("chan")
    y, x = c // 2, lax.rem(c, 2)
    up, down = lax.rem(d + 1, ND), lax.rem(d + ND - 1, ND)
    other = c ^ 1

    loads = [
        pltpu.make_async_copy(slopes_in, slopes_all.at[2 + x], local_sem.at[0]),
        pltpu.make_async_copy(act_in, act_all.at[y], local_sem.at[1]),
        pltpu.make_async_copy(weight_in, weight_v, local_sem.at[2]),
    ]
    half_x, z, core = d // 32, lax.rem(d // 2, NZ), lax.rem(d, 2)
    chan_peers = [(d, lax.rem(c + k, NC)) for k in CHAN_OFFSETS]
    near = [(up, c), (down, c), (up, other), (down, other)]
    owner = z == 0
    barrier = pltpu.get_barrier_semaphore()

    def greet(peer):
        pl.semaphore_signal(barrier, inc=1, device_id=peer, device_id_type=MESH)

    def beside(k):
        return d, lax.rem(c + 2 * k + NC, NC)

    close = [beside(k) for k in (-2, 2, -1, 1)] + [(d, other), (d ^ 32, c), (d ^ 33, c), (down, c), (down, other)]
    seam = jnp.logical_and(owner, core == 0)
    tail = jnp.logical_and(z == NZ - 1, core == 1)
    for peer in close:
        greet(peer)

    @pl.when(jnp.logical_not(tail))
    def _():
        greet((up, c))
        greet((up, other))

    @pl.when(seam)
    def _():
        for k in range(1, 8):
            greet((down, lax.rem(c + 2 * k, NC)))

    @pl.when(owner)
    def _():
        for level in range(1, NZ):
            greet((half_x * 32 + level * 2 + core, c))

    for load in loads:
        load.start()

    def send(src, dst, group, peer):
        pltpu.make_async_remote_copy(
            src_ref=src, dst_ref=dst, send_sem=send_sem.at[group],
            recv_sem=recv_sem.at[group], device_id=peer, device_id_type=MESH,
        ).start()

    loads[0].wait()
    loads[1].wait()

    @pl.when(seam)
    def _():
        pl.semaphore_wait(barrier, 9)

    @pl.when(jnp.logical_and(owner, core == 1))
    def _():
        pl.semaphore_wait(barrier, 11)

    @pl.when(tail)
    def _():
        pl.semaphore_wait(barrier, 19)

    @pl.when(jnp.logical_not(jnp.logical_or(owner, tail)))
    def _():
        pl.semaphore_wait(barrier, 12)

    def block(k):
        return lax.rem(y + k + 8, 8)

    for group, k in ((0, 2), (1, -2)):
        send(act_all.at[y], act_all.at[y], group, beside(k))
    own = slopes_all.at[2 + x]
    send(own, slopes_all.at[2 + x], 18, (d, other))
    send(own, slopes_all.at[4 + x], 12, (up, c))

    @pl.when(core == 1)
    def _():
        send(own, slopes_all.at[4 + x], 20, (up, other))

    @pl.when(jnp.logical_and(core == 0, jnp.logical_not(seam)))
    def _():
        send(own, slopes_all.at[x], 19, (down, other))

    @pl.when(jnp.logical_not(seam))
    def _():
        send(own, slopes_all.at[x], 3, (down, c))

    @pl.when(tail)
    def _():
        for k in (4, 3, 5, 2, 6, 1, 7, 0):
            send(act_all.at[y], seam_act.at[y], 16, (up, lax.rem(c + 2 * k, NC)))

    act_taps[0:32, 128:256] = jnp.zeros((32, 128), BF16)
    act_taps[64:96, 4096:4224] = jnp.zeros((32, 128), BF16)
    terms[...] = jnp.zeros((160, 128), F32)
    source = lax.broadcasted_iota(jnp.int32, (256, 256), 0)
    target = lax.broadcasted_iota(jnp.int32, (256, 256), 1)
    slot = (target & 3) * 8 + ((target & 63) >> 3) + ((target >> 6) * 32) + ((target >> 2) & 1) * 128
    spread[...] = jnp.where(source == slot, 1.0, 0.0).astype(BF16)

    def convert(k):
        at = block(k)
        act_f[pl.ds(pl.multiple_of(at * 128, 128), 128)] = act_all[at].astype(F32)

    def hand_on(group, k):
        drained(act_all.at[0], recv_sem.at[group])
        behind = block(-k)
        part = pl.ds(0 if k > 0 else 64, 64)
        send(act_all.at[behind, part], act_all.at[behind, part], 4, beside(k))
        send(act_all.at[behind], act_all.at[behind], 4, beside(k // 2))

    from_below = jnp.logical_and(y >= 2, y < 6)

    @pl.when(from_below)
    def _():
        hand_on(0, 2)
        hand_on(1, -2)

    @pl.when(jnp.logical_not(from_below))
    def _():
        hand_on(1, -2)
        hand_on(0, 2)

    for k in (1, -1):
        send(act_all.at[y], act_all.at[y], 2, beside(k))

    drained(own, recv_sem.at[18])
    across = slopes_all.at[3 - x]

    @pl.when(core == 0)
    def _():
        send(across, slopes_all.at[5 - x], 20, (up, c))

    @pl.when(core == 1)
    def _():
        send(across, slopes_all.at[1 - x], 19, (down, c))

    for k in (0, 2, -2):
        convert(k)

    has_up = jnp.where(d == ND - 1, 0.0, 1.0).astype(F32)
    has_down = jnp.where(d == 0, 0.0, 1.0).astype(F32)
    zero8 = jnp.zeros((8, 128), F32)

    def column_slopes(rel, up_group, down_group):
        xx = x if rel == 0 else 1 - x

        @pl.when(jnp.logical_not(tail))
        def _():
            drained(own, recv_sem.at[up_group])

        drained(own, recv_sem.at[down_group])
        for a in range(3):
            value = slopes_all[2 * a + xx].astype(F32)
            if a == 0:
                value = jnp.where(tail, 0.0, value)
            if a == 2:
                value = value * has_down
            slopes_f[(2 * a + rel) * 256:(2 * a + rel + 1) * 256] = value

        def slope_rows(step, carry):
            for part in range(4):
                h = step * 4 + part
                at = pl.ds(pl.multiple_of(h * 128, 128), 128)
                shifted = []
                for a in range(3):
                    row = slopes_f[pl.ds((2 * a + rel) * 256 + h, 8, stride=32), :]
                    left = jnp.where(lane8 == 127, 0.0, pltpu.roll(row, 127, 1))
                    right = jnp.where(lane8 == 0, 0.0, pltpu.roll(row, 1, 1))
                    shifted += [left, row, right]
                shifted.append(zero8)
                for t in range(5):
                    at_row = rel * 80 + t * 16
                    both = jnp.concatenate(shifted[2 * t:2 * t + 2], axis=0)
                    taps[at_row:at_row + 16, at] = both.astype(BF16)
            return carry

        lax.fori_loop(0, 8, slope_rows, 0)

    lane8 = lax.broadcasted_iota(jnp.int32, (8, 128), 1)
    column_slopes(0, 3, 12)

    def fill_rows(blocks, plane):
        def row(h):
            return slopes_f[pl.ds(plane * 256 + h, 8, stride=32), :] if 0 <= h < 32 else zero8

        for p in range(NC):
            block = [row(2 * p - 1 + j) for j in range(4)]
            blocks[p] = jnp.concatenate(block, axis=0).astype(BF16)

    fill_rows(rows_send, 2)
    rows_recv[c] = rows_send[c]
    column_slopes(1, 19, 20)

    drained(act_all.at[pl.ds(0, 2)], recv_sem.at[2])
    convert(1)
    convert(-1)
    drained(act_all.at[pl.ds(0, 3)], recv_sem.at[4])

    def send_rows():
        for peer in chan_peers:
            send(rows_send.at[peer[1]], rows_recv.at[c], 5, peer)

    @pl.when(seam)
    def _():
        send_rows()
        fill_rows(seam_send, 4)
        seam_recv[c] = seam_send[c]
        for peer in chan_peers:
            send(seam_send.at[peer[1]], seam_recv.at[c], 15, peer)

    for k in (3, -3, 4):
        convert(k)

    def act_rows(step, carry):
        for part in range(4):
            h = step * 4 + part
            row = jnp.concatenate(
                [act_f[pl.ds(i * 32 + h, 8, stride=128), :] for i in range(4)], axis=0
            ).astype(BF16)
            for b in range(3):
                at = pl.ds(pl.multiple_of((h + 2 - b) * 128, 128), 128)
                act_taps[b * 32:(b + 1) * 32, at] = row
        return carry

    lax.fori_loop(0, 8, act_rows, 0)

    def filter_terms(rows):
        return lax.dot_general(
            rows, act_taps[0:96, 128:4224], (((1,), (1,)), ((), ())), preferred_element_type=F32
        )

    place = 2 * half_x + core

    def pack_and_send(to_core):
        rel = x if to_core == 1 else 1 - x

        def tile(a, third):
            return terms[pl.ds(pl.multiple_of(rel * 80 + (3 * a + third) * 8, 8), 8)]

        packed = []
        for a in range(3):
            last = tile(a, 2)
            packed.append(jnp.where(lane8 < 96, tile(a, 0), pltpu.roll(last, 96, 1)))
            packed.append(jnp.where(lane8 < 96, tile(a, 1), pltpu.roll(last, 64, 1)))
        rest = jnp.zeros((8, 128), F32)
        for a in range(3):
            part = pltpu.roll(tile(a, 2), (32 * a - 64) % 128, 1)
            rest = jnp.where((lane8 >= 32 * a) & (lane8 < 32 * a + 32), part, rest)
        packed.append(rest)
        for h in range(NX):
            quad_send[h, to_core, 0:24] = jnp.concatenate(packed[4 * h:4 * h + 3], axis=0)
            quad_send[h, to_core, 24:28] = packed[3][4 * h:4 * h + 4]
        here = d - core + to_core
        send(quad_send.at[1 - half_x, to_core], quad_recv.at[place], 6, (here ^ 32, c))

        @pl.when(to_core != core)
        def _():
            send(quad_send.at[half_x, to_core], quad_recv.at[place], 6, (d ^ 1, c))

    terms[:, 0:96] = filter_terms(taps[...])

    @pl.when(d != ND // 2)
    def _():
        for to_core in (1, 0):
            pack_and_send(to_core)

    pl.when(jnp.logical_not(seam))(send_rows)

    @pl.when(d == ND // 2)
    def _():
        drained(seam_act, recv_sem.at[16])
        for p in range(8):
            act_f[p * 128:(p + 1) * 128] = seam_act[p].astype(F32)
        lax.fori_loop(0, 8, act_rows, 0)
        extra = filter_terms(taps[16:128])
        for rel in range(2):
            at_row = rel * 80
            terms[at_row:at_row + 24, 0:96] = terms[at_row:at_row + 24, 0:96] + extra[at_row + 8:at_row + 32]
        for to_core in (1, 0):
            pack_and_send(to_core)

    quad_recv[place] = quad_send[half_x, core]

    @pl.when(jnp.logical_not(owner))
    def _():
        drained(quad_recv.at[pl.ds(0, 3)], recv_sem.at[6])
        quarter[...] = (quad_recv[0] + quad_recv[1]) + (quad_recv[2] + quad_recv[3])

    @pl.when(jnp.logical_and(z > 0, z < LATE))
    def _():
        send(quarter, piece_recv.at[z], 7, (half_x * 32 + core, c))

    @pl.when(z >= LATE)
    def _():
        send(quarter, piece_recv.at[z], 8, (half_x * 32 + core, c))

    loads[2].wait()
    drained(rows_recv.at[pl.ds(0, 15)], recv_sem.at[5])
    lane128 = lax.broadcasted_iota(jnp.int32, (128, 128), 1)

    def column_taps(blocks):
        for j in range(4):
            row = blocks[:, j * 8:(j + 1) * 8, :].astype(F32).reshape(128, 128)
            left = jnp.where(lane128 == 127, 0.0, pltpu.roll(row, 127, 1))
            right = jnp.where(lane128 == 0, 0.0, pltpu.roll(row, 1, 1))
            for third, value in enumerate((left, row, right)):
                rows_taps[third * 128:(third + 1) * 128, j * 128:(j + 1) * 128] = value.astype(BF16)

    def plane_term(a):
        left_side = jnp.concatenate(
            [weight_v[(9 * a + k) * 64:(9 * a + k + 1) * 64] for k in range(9)], axis=1
        )
        right_side = jnp.concatenate(
            [rows_taps[:, (2 - b) * 128:(4 - b) * 128] for b in range(3)], axis=0
        )
        return jnp.dot(left_side, right_side, preferred_element_type=F32)

    column_taps(rows_recv)
    near_send[0] = plane_term(0)
    send(near_send.at[0], near_recv.at[0], 9, (down, c))
    near_send[1] = plane_term(2)

    @pl.when(jnp.logical_not(tail))
    def _():
        send(near_send.at[1], near_recv.at[1], 14, (up, c))

    whole_sum[...] = plane_term(1)

    @pl.when(seam)
    def _():
        drained(seam_recv.at[pl.ds(0, 15)], recv_sem.at[15])
        column_taps(seam_recv)
        near_recv[1] = plane_term(2)

    @pl.when(jnp.logical_not(seam))
    def _():
        drained(near_recv.at[1], recv_sem.at[14])

    drained(near_recv.at[0], recv_sem.at[9])
    whole = whole_sum[...] + near_recv[0] * has_up + near_recv[1] * has_down
    for p in range(NC):
        back_send[p * 8:(p + 1) * 8] = jnp.concatenate(
            [whole[4 * p:4 * p + 4, 0:128], whole[4 * p:4 * p + 4, 128:256]], axis=0
        )
    mine = pl.ds(pl.multiple_of(c * 8, 8), 8)
    back_recv[mine] = back_send[mine]
    for peer in chan_peers:
        theirs = pl.ds(pl.multiple_of(peer[1] * 8, 8), 8)
        send(back_send.at[theirs], back_recv.at[mine], 10, peer)

    goal = c - x + 1 - core

    @pl.when(owner)
    def _():
        drained(quad_recv.at[pl.ds(0, 3)], recv_sem.at[6])
        total = (quad_recv[0] + quad_recv[1]) + (quad_recv[2] + quad_recv[3])
        drained(piece_recv.at[pl.ds(0, LATE - 1)], recv_sem.at[7])
        for k in range(1, LATE):
            total = total + piece_recv[k]
        drained(piece_recv.at[pl.ds(0, NZ - LATE)], recv_sem.at[8])
        for k in range(LATE, NZ):
            total = total + piece_recv[k]
        piece_sum[...] = total

        def give(peer):
            send(piece_sum, gathered.at[half_x, x], 11, peer)

        give((d ^ 32, goal))
        give((d ^ 33, goal))
        give((d ^ 1, goal))

        @pl.when(goal == c)
        def _():
            gathered[half_x, x] = total

        @pl.when(goal != c)
        def _():
            give((d, goal))

        for level, _ in HAND_ON:
            for hop in (1, 0):
                give(((half_x ^ hop) * 32 + level * 2 + half_x, goal))

    drained(back_recv.at[pl.ds(0, 120)], recv_sem.at[10])
    for i in range(4):
        grad_out[i] = back_recv[pl.ds(i, 32, stride=4), :].astype(BF16)

    kept = jnp.logical_and(owner, goal == c)

    @pl.when(kept)
    def _():
        drained(piece_recv.at[pl.ds(0, 3)], recv_sem.at[11])

    @pl.when(jnp.logical_and(owner, goal != c))
    def _():
        drained(piece_recv.at[pl.ds(0, 4)], recv_sem.at[11])

    @pl.when(jnp.logical_not(owner))
    def _():
        drained(piece_recv.at[pl.ds(0, 2)], recv_sem.at[11])
        send(gathered.at[core], gathered.at[core], 13, (d ^ 1, c))
        for level, followers in [pair for pair in HAND_ON if pair[1]]:
            @pl.when(z == level)
            def _():
                for follower in followers:
                    send(gathered.at[core], gathered.at[core], 11, (half_x * 32 + follower * 2 + core, c))

        drained(gathered.at[1 - core], recv_sem.at[13])

    sides = [
        jnp.concatenate(
            [gathered[0, xx, 0:24], gathered[0, xx, 24:28], gathered[1, xx, 24:28], gathered[1, xx, 0:24]], axis=0
        )
        for xx in range(2)
    ]
    both = jnp.concatenate(sides, axis=1)
    high = both.astype(BF16)
    rest = both - high.astype(F32)
    mid = rest.astype(BF16)
    low = (rest - mid.astype(F32)).astype(BF16)
    split = jnp.concatenate([high.astype(F32), mid.astype(F32), low.astype(F32)], axis=0).astype(BF16)
    placed = jnp.dot(split, spread[...], preferred_element_type=F32)
    result = ((placed[0:56] + placed[56:112]) + placed[112:168]) * (1.0 / math.sqrt(ND * 32 * 128))
    for a in range(3):
        for b in range(3):
            for third in range(3):
                if third < 2:
                    t, part = 2 * a + third, b
                elif b < 2:
                    t, part = 2 * a + b, 3
                else:
                    t, part = 6, a
                filt_out[9 * a + 3 * b + third] = result[t * 8:t * 8 + 8, part * 64:part * 64 + 64]

    @pl.when(d == 0)
    def _():
        drained(seam_act, recv_sem.at[16])

    for group in (0, 1):
        drained(act_all.at[0], send_sem.at[group])
    drained(act_all.at[pl.ds(0, 2)], send_sem.at[2])
    for group in (12, 18, 20):
        drained(own, send_sem.at[group])
    drained(act_all.at[pl.ds(0, 3)], send_sem.at[4])
    drained(rows_recv.at[pl.ds(0, 15)], send_sem.at[5])
    drained(quad_recv.at[pl.ds(0, 3)], send_sem.at[6])
    drained(near_send.at[0], send_sem.at[9])
    drained(back_send.at[pl.ds(0, 120)], send_sem.at[10])

    @pl.when(seam)
    def _():
        drained(seam_recv.at[pl.ds(0, 15)], send_sem.at[15])

    @pl.when(jnp.logical_not(seam))
    def _():
        drained(own, send_sem.at[3])
        drained(own, send_sem.at[19])

    @pl.when(tail)
    def _():
        drained(seam_act, send_sem.at[16])

    @pl.when(jnp.logical_not(tail))
    def _():
        drained(near_send.at[1], send_sem.at[14])

    @pl.when(jnp.logical_and(z > 0, z < LATE))
    def _():
        drained(quarter, send_sem.at[7])

    @pl.when(z >= LATE)
    def _():
        drained(quarter, send_sem.at[8])

    @pl.when(owner)
    def _():
        drained(piece_recv.at[pl.ds(0, 3 + 2 * len(HAND_ON))], send_sem.at[11])

    @pl.when(jnp.logical_and(owner, goal != c))
    def _():
        drained(piece_recv.at[0], send_sem.at[11])

    @pl.when(jnp.logical_not(owner))
    def _():
        drained(gathered.at[0], send_sem.at[13])

    for level, followers in [pair for pair in HAND_ON if pair[1]]:
        @pl.when(z == level)
        def _():
            drained(piece_recv.at[pl.ds(0, 2 * len(followers))], send_sem.at[11])


def write_out(grad_in, filt_in, grad_out, filt_out):
    grad_out[...] = grad_in[...]
    filt_out[...] = filt_in[...]


def per_device(activations, slopes, weight):
    hbm = pl.BlockSpec(memory_space=pltpu.HBM)
    vmem = pl.BlockSpec(memory_space=pltpu.VMEM)
    grad, filt = pl.pallas_call(
        kernel,
        name="conv_grads",
        out_shape=(pltpu.VMEM((4, 32, 128), BF16), pltpu.VMEM((27, 8, 64), F32)),
        in_specs=[hbm] * 3,
        out_specs=(vmem, vmem),
        scratch_shapes=[
            pltpu.VMEM((8, 128, 128), BF16),
            pltpu.VMEM((8, 128, 128), BF16),
            pltpu.VMEM((160, 128), F32),
            pltpu.VMEM((6, 256, 128), BF16),
            pltpu.VMEM((27 * 64, 128), BF16),
            pltpu.VMEM((6 * 256 + 32, 128), F32),
            pltpu.VMEM((9 * 128, 128), F32),
            pltpu.VMEM((160, 32 * 128), BF16),
            pltpu.VMEM((96, 34 * 128), BF16),
            pltpu.VMEM((NC, 32, 128), BF16),
            pltpu.VMEM((NC, 32, 128), BF16),
            pltpu.VMEM((NC, 32, 128), BF16),
            pltpu.VMEM((NC, 32, 128), BF16),
            pltpu.VMEM((384, 512), BF16),
            pltpu.VMEM((2, 64, 256), F32),
            pltpu.VMEM((2, 64, 256), F32),
            pltpu.VMEM((64, 256), F32),
            pltpu.VMEM((128, 128), F32),
            pltpu.VMEM((136, 128), F32),
            pltpu.VMEM((NX, 2, 28, 128), F32),
            pltpu.VMEM((4, 28, 128), F32),
            pltpu.VMEM((28, 128), F32),
            pltpu.VMEM((NZ, 28, 128), F32),
            pltpu.VMEM((28, 128), F32),
            pltpu.VMEM((2, 2, 28, 128), F32),
            pltpu.VMEM((256, 256), BF16),
            pltpu.SemaphoreType.DMA((3,)),
            pltpu.SemaphoreType.DMA((21,)),
            pltpu.SemaphoreType.DMA((21,)),
        ],
        compiler_params=pltpu.CompilerParams(
            collective_id=0, has_side_effects=True, vmem_limit_bytes=32 * 1024 * 1024
        ),
    )(
        pltpu.with_memory_space_constraint(activations.reshape(128, 128), pltpu.HBM),
        pltpu.with_memory_space_constraint(slopes.reshape(256, 128), pltpu.HBM),
        pltpu.with_memory_space_constraint(weight.reshape(27 * 64, 128), pltpu.HBM),
    )
    grad, filt = pl.pallas_call(
        write_out,
        name="write_out",
        out_shape=(
            jax.ShapeDtypeStruct((4, 32, 128), BF16),
            jax.ShapeDtypeStruct((27, 8, 64), F32),
        ),
        in_specs=[vmem] * 2,
        out_specs=(vmem, vmem),
    )(pltpu.with_memory_space_constraint(grad, pltpu.VMEM), pltpu.with_memory_space_constraint(filt, pltpu.VMEM))
    return grad.reshape(4, 1, 32, 128), jnp.transpose(filt, (0, 2, 1))


def solution(mesh):
    placed = (P("chan", "depth", None, None), P("chan", "depth", None, None), P())
    return jax.shard_map(
        per_device,
        mesh=mesh,
        in_specs=placed,
        out_specs=(P("chan", "depth", None, None), P(None, None, "chan")),
        check_vma=False,
    )
```

```python
import math

import jax
import jax.numpy as jnp
from jax import lax
from jax.experimental import pallas as pl
from jax.experimental.pallas import tpu as pltpu
from jax.sharding import PartitionSpec as P

MESH = pl.DeviceIdType.MESH
F32, BF16 = jnp.float32, jnp.bfloat16
ND, NC = 64, 16
NZ = 16
NX = 2
LATE = 12
HAND_ON = ((1, ()), (2, ()), (3, ()), (4, ()), (5, (6, 7, 8)), (15, (14, 13, 12, 11, 10, 9)))
CHAN_OFFSETS = (8, 9, 6, 10, 7, 11, 4, 12, 5, 13, 2, 14, 3, 15, 1)


def drained(ref, sem):
    pltpu.make_async_copy(ref, ref, sem).wait()


def kernel(
    act_in, slopes_in, weight_in,
    grad_out, filt_out,
    act_all, seam_act, terms, slopes_all, weight_v, slopes_f, act_f, taps, act_taps,
    rows_send, rows_recv, seam_send, seam_recv, rows_taps, near_send, near_recv, whole_sum, back_send, back_recv,
    quad_send, quad_recv, quarter, piece_recv, piece_sum, gathered, spread,
    local_sem, send_sem, recv_sem,
):
    d, c = lax.axis_index("depth"), lax.axis_index("chan")
    y, x = c // 2, lax.rem(c, 2)
    up, down = lax.rem(d + 1, ND), lax.rem(d + ND - 1, ND)
    other = c ^ 1

    loads = [
        pltpu.make_async_copy(slopes_in, slopes_all.at[2 + x], local_sem.at[0]),
        pltpu.make_async_copy(act_in, act_all.at[y], local_sem.at[1]),
        pltpu.make_async_copy(weight_in, weight_v, local_sem.at[2]),
    ]
    half_x, z, core = d // 32, lax.rem(d // 2, NZ), lax.rem(d, 2)
    chan_peers = [(d, lax.rem(c + k, NC)) for k in CHAN_OFFSETS]
    near = [(up, c), (down, c), (up, other), (down, other)]
    owner = z == 0
    barrier = pltpu.get_barrier_semaphore()

    def greet(peer):
        pl.semaphore_signal(barrier, inc=1, device_id=peer, device_id_type=MESH)

    def beside(k):
        return d, lax.rem(c + 2 * k + NC, NC)

    close = [beside(k) for k in (-2, 2, -1, 1)] + [(d, other), (d ^ 32, c), (d ^ 33, c), (down, c), (down, other)]
    seam = jnp.logical_and(owner, core == 0)
    tail = jnp.logical_and(z == NZ - 1, core == 1)
    for peer in close:
        greet(peer)

    @pl.when(jnp.logical_not(tail))
    def _():
        greet((up, c))
        greet((up, other))

    @pl.when(seam)
    def _():
        for k in range(1, 8):
            greet((down, lax.rem(c + 2 * k, NC)))

    @pl.when(owner)
    def _():
        for level in range(1, NZ):
            greet((half_x * 32 + level * 2 + core, c))

    for load in loads:
        load.start()

    def send(src, dst, group, peer):
        pltpu.make_async_remote_copy(
            src_ref=src, dst_ref=dst, send_sem=send_sem.at[group],
            recv_sem=recv_sem.at[group], device_id=peer, device_id_type=MESH,
        ).start()

    loads[0].wait()
    loads[1].wait()

    @pl.when(seam)
    def _():
        pl.semaphore_wait(barrier, 9)

    @pl.when(jnp.logical_and(owner, core == 1))
    def _():
        pl.semaphore_wait(barrier, 11)

    @pl.when(tail)
    def _():
        pl.semaphore_wait(barrier, 19)

    @pl.when(jnp.logical_not(jnp.logical_or(owner, tail)))
    def _():
        pl.semaphore_wait(barrier, 12)

    def block(k):
        return lax.rem(y + k + 8, 8)

    for group, k in ((0, 2), (1, -2)):
        send(act_all.at[y], act_all.at[y], group, beside(k))
    own = slopes_all.at[2 + x]
    send(own, slopes_all.at[2 + x], 18, (d, other))
    send(own, slopes_all.at[4 + x], 12, (up, c))

    @pl.when(core == 1)
    def _():
        send(own, slopes_all.at[4 + x], 20, (up, other))

    @pl.when(jnp.logical_and(core == 0, jnp.logical_not(seam)))
    def _():
        send(own, slopes_all.at[x], 19, (down, other))

    @pl.when(jnp.logical_not(seam))
    def _():
        send(own, slopes_all.at[x], 3, (down, c))

    @pl.when(tail)
    def _():
        for k in (4, 3, 5, 2, 6, 1, 7, 0):
            send(act_all.at[y], seam_act.at[y], 16, (up, lax.rem(c + 2 * k, NC)))

    act_taps[0:32, 128:256] = jnp.zeros((32, 128), BF16)
    act_taps[64:96, 4096:4224] = jnp.zeros((32, 128), BF16)
    terms[...] = jnp.zeros((160, 128), F32)
    source = lax.broadcasted_iota(jnp.int32, (256, 256), 0)
    target = lax.broadcasted_iota(jnp.int32, (256, 256), 1)
    slot = (target & 3) * 8 + ((target & 63) >> 3) + ((target >> 6) * 32) + ((target >> 2) & 1) * 128
    spread[...] = jnp.where(source == slot, 1.0, 0.0).astype(BF16)

    def convert(k):
        at = block(k)
        act_f[pl.ds(pl.multiple_of(at * 128, 128), 128)] = act_all[at].astype(F32)

    def hand_on(group, k):
        drained(act_all.at[0], recv_sem.at[group])
        behind = block(-k)
        part = pl.ds(0 if k > 0 else 64, 64)
        send(act_all.at[behind, part], act_all.at[behind, part], 4, beside(k))
        send(act_all.at[behind], act_all.at[behind], 4, beside(k // 2))

    from_below = jnp.logical_and(y >= 2, y < 6)

    @pl.when(from_below)
    def _():
        hand_on(0, 2)
        hand_on(1, -2)

    @pl.when(jnp.logical_not(from_below))
    def _():
        hand_on(1, -2)
        hand_on(0, 2)

    for k in (1, -1):
        send(act_all.at[y], act_all.at[y], 2, beside(k))

    drained(own, recv_sem.at[18])
    across = slopes_all.at[3 - x]

    @pl.when(core == 0)
    def _():
        send(across, slopes_all.at[5 - x], 20, (up, c))

    @pl.when(core == 1)
    def _():
        send(across, slopes_all.at[1 - x], 19, (down, c))

    for k in (0, 2, -2):
        convert(k)

    has_up = jnp.where(d == ND - 1, 0.0, 1.0).astype(F32)
    has_down = jnp.where(d == 0, 0.0, 1.0).astype(F32)
    zero8 = jnp.zeros((8, 128), F32)

    def column_slopes(rel, up_group, down_group):
        xx = x if rel == 0 else 1 - x

        @pl.when(jnp.logical_not(tail))
        def _():
            drained(own, recv_sem.at[up_group])

        drained(own, recv_sem.at[down_group])
        for a in range(3):
            value = slopes_all[2 * a + xx].astype(F32)
            if a == 0:
                value = jnp.where(tail, 0.0, value)
            if a == 2:
                value = value * has_down
            slopes_f[(2 * a + rel) * 256:(2 * a + rel + 1) * 256] = value

        def slope_rows(step, carry):
            for part in range(4):
                h = step * 4 + part
                at = pl.ds(pl.multiple_of(h * 128, 128), 128)
                shifted = []
                for a in range(3):
                    row = slopes_f[pl.ds((2 * a + rel) * 256 + h, 8, stride=32), :]
                    left = jnp.where(lane8 == 127, 0.0, pltpu.roll(row, 127, 1))
                    right = jnp.where(lane8 == 0, 0.0, pltpu.roll(row, 1, 1))
                    shifted += [left, row, right]
                shifted.append(zero8)
                for t in range(5):
                    at_row = rel * 80 + t * 16
                    both = jnp.concatenate(shifted[2 * t:2 * t + 2], axis=0)
                    taps[at_row:at_row + 16, at] = both.astype(BF16)
            return carry

        lax.fori_loop(0, 8, slope_rows, 0)

    lane8 = lax.broadcasted_iota(jnp.int32, (8, 128), 1)
    column_slopes(0, 3, 12)

    def fill_rows(blocks, plane):
        def row(h):
            return slopes_f[pl.ds(plane * 256 + h, 8, stride=32), :] if 0 <= h < 32 else zero8

        for p in range(NC):
            block = [row(2 * p - 1 + j) for j in range(4)]
            blocks[p] = jnp.concatenate(block, axis=0).astype(BF16)

    fill_rows(rows_send, 2)
    rows_recv[c] = rows_send[c]
    column_slopes(1, 19, 20)

    drained(act_all.at[pl.ds(0, 2)], recv_sem.at[2])
    convert(1)
    convert(-1)
    drained(act_all.at[pl.ds(0, 3)], recv_sem.at[4])

    def send_rows():
        for peer in chan_peers:
            send(rows_send.at[peer[1]], rows_recv.at[c], 5, peer)

    @pl.when(seam)
    def _():
        send_rows()
        fill_rows(seam_send, 4)
        seam_recv[c] = seam_send[c]
        for peer in chan_peers:
            send(seam_send.at[peer[1]], seam_recv.at[c], 15, peer)

    for k in (3, -3, 4):
        convert(k)

    def act_rows(step, carry):
        for part in range(4):
            h = step * 4 + part
            row = jnp.concatenate(
                [act_f[pl.ds(i * 32 + h, 8, stride=128), :] for i in range(4)], axis=0
            ).astype(BF16)
            for b in range(3):
                at = pl.ds(pl.multiple_of((h + 2 - b) * 128, 128), 128)
                act_taps[b * 32:(b + 1) * 32, at] = row
        return carry

    lax.fori_loop(0, 8, act_rows, 0)

    def filter_terms(rows):
        return lax.dot_general(
            rows, act_taps[0:96, 128:4224], (((1,), (1,)), ((), ())), preferred_element_type=F32
        )

    place = 2 * half_x + core

    def pack_and_send(to_core):
        rel = x if to_core == 1 else 1 - x

        def tile(a, third):
            return terms[pl.ds(pl.multiple_of(rel * 80 + (3 * a + third) * 8, 8), 8)]

        packed = []
        for a in range(3):
            last = tile(a, 2)
            packed.append(jnp.where(lane8 < 96, tile(a, 0), pltpu.roll(last, 96, 1)))
            packed.append(jnp.where(lane8 < 96, tile(a, 1), pltpu.roll(last, 64, 1)))
        rest = jnp.zeros((8, 128), F32)
        for a in range(3):
            part = pltpu.roll(tile(a, 2), (32 * a - 64) % 128, 1)
            rest = jnp.where((lane8 >= 32 * a) & (lane8 < 32 * a + 32), part, rest)
        packed.append(rest)
        for h in range(NX):
            quad_send[h, to_core, 0:24] = jnp.concatenate(packed[4 * h:4 * h + 3], axis=0)
            quad_send[h, to_core, 24:28] = packed[3][4 * h:4 * h + 4]
        here = d - core + to_core
        send(quad_send.at[1 - half_x, to_core], quad_recv.at[place], 6, (here ^ 32, c))

        @pl.when(to_core != core)
        def _():
            send(quad_send.at[half_x, to_core], quad_recv.at[place], 6, (d ^ 1, c))

    terms[:, 0:96] = filter_terms(taps[...])

    @pl.when(d != ND // 2)
    def _():
        for to_core in (1, 0):
            pack_and_send(to_core)

    pl.when(jnp.logical_not(seam))(send_rows)

    @pl.when(d == ND // 2)
    def _():
        drained(seam_act, recv_sem.at[16])
        for p in range(8):
            act_f[p * 128:(p + 1) * 128] = seam_act[p].astype(F32)
        lax.fori_loop(0, 8, act_rows, 0)
        extra = filter_terms(taps[16:128])
        for rel in range(2):
            at_row = rel * 80
            terms[at_row:at_row + 24, 0:96] = terms[at_row:at_row + 24, 0:96] + extra[at_row + 8:at_row + 32]
        for to_core in (1, 0):
            pack_and_send(to_core)

    quad_recv[place] = quad_send[half_x, core]

    @pl.when(jnp.logical_not(owner))
    def _():
        drained(quad_recv.at[pl.ds(0, 3)], recv_sem.at[6])
        quarter[...] = (quad_recv[0] + quad_recv[1]) + (quad_recv[2] + quad_recv[3])

    @pl.when(jnp.logical_and(z > 0, z < LATE))
    def _():
        send(quarter, piece_recv.at[z], 7, (half_x * 32 + core, c))

    @pl.when(z >= LATE)
    def _():
        send(quarter, piece_recv.at[z], 8, (half_x * 32 + core, c))

    loads[2].wait()
    drained(rows_recv.at[pl.ds(0, 15)], recv_sem.at[5])
    lane128 = lax.broadcasted_iota(jnp.int32, (128, 128), 1)

    def column_taps(blocks):
        for j in range(4):
            row = blocks[:, j * 8:(j + 1) * 8, :].astype(F32).reshape(128, 128)
            left = jnp.where(lane128 == 127, 0.0, pltpu.roll(row, 127, 1))
            right = jnp.where(lane128 == 0, 0.0, pltpu.roll(row, 1, 1))
            for third, value in enumerate((left, row, right)):
                rows_taps[third * 128:(third + 1) * 128, j * 128:(j + 1) * 128] = value.astype(BF16)

    def plane_term(a):
        left_side = jnp.concatenate(
            [weight_v[(9 * a + k) * 64:(9 * a + k + 1) * 64] for k in range(9)], axis=1
        )
        right_side = jnp.concatenate(
            [rows_taps[:, (2 - b) * 128:(4 - b) * 128] for b in range(3)], axis=0
        )
        return jnp.dot(left_side, right_side, preferred_element_type=F32)

    column_taps(rows_recv)
    near_send[0] = plane_term(0)
    send(near_send.at[0], near_recv.at[0], 9, (down, c))
    near_send[1] = plane_term(2)

    @pl.when(jnp.logical_not(tail))
    def _():
        send(near_send.at[1], near_recv.at[1], 14, (up, c))

    whole_sum[...] = plane_term(1)

    @pl.when(seam)
    def _():
        drained(seam_recv.at[pl.ds(0, 15)], recv_sem.at[15])
        column_taps(seam_recv)
        near_recv[1] = plane_term(2)

    @pl.when(jnp.logical_not(seam))
    def _():
        drained(near_recv.at[1], recv_sem.at[14])

    drained(near_recv.at[0], recv_sem.at[9])
    whole = whole_sum[...] + near_recv[0] * has_up + near_recv[1] * has_down
    for p in range(NC):
        back_send[p * 8:(p + 1) * 8] = jnp.concatenate(
            [whole[4 * p:4 * p + 4, 0:128], whole[4 * p:4 * p + 4, 128:256]], axis=0
        )
    mine = pl.ds(pl.multiple_of(c * 8, 8), 8)
    back_recv[mine] = back_send[mine]
    for peer in chan_peers:
        theirs = pl.ds(pl.multiple_of(peer[1] * 8, 8), 8)
        send(back_send.at[theirs], back_recv.at[mine], 10, peer)

    goal = c - x + 1 - core

    @pl.when(owner)
    def _():
        drained(quad_recv.at[pl.ds(0, 3)], recv_sem.at[6])
        total = (quad_recv[0] + quad_recv[1]) + (quad_recv[2] + quad_recv[3])
        drained(piece_recv.at[pl.ds(0, LATE - 1)], recv_sem.at[7])
        for k in range(1, LATE):
            total = total + piece_recv[k]
        drained(piece_recv.at[pl.ds(0, NZ - LATE)], recv_sem.at[8])
        for k in range(LATE, NZ):
            total = total + piece_recv[k]
        piece_sum[...] = total

        def give(peer):
            send(piece_sum, gathered.at[half_x, x], 11, peer)

        give((d ^ 32, goal))
        give((d ^ 33, goal))
        give((d ^ 1, goal))

        @pl.when(goal == c)
        def _():
            gathered[half_x, x] = total

        @pl.when(goal != c)
        def _():
            give((d, goal))

        for level, _ in HAND_ON:
            for hop in (1, 0):
                give(((half_x ^ hop) * 32 + level * 2 + half_x, goal))

    drained(back_recv.at[pl.ds(0, 120)], recv_sem.at[10])
    for i in range(4):
        grad_out[i] = back_recv[pl.ds(i, 32, stride=4), :].astype(BF16)

    kept = jnp.logical_and(owner, goal == c)

    @pl.when(kept)
    def _():
        drained(piece_recv.at[pl.ds(0, 3)], recv_sem.at[11])

    @pl.when(jnp.logical_and(owner, goal != c))
    def _():
        drained(piece_recv.at[pl.ds(0, 4)], recv_sem.at[11])

    @pl.when(jnp.logical_not(owner))
    def _():
        drained(piece_recv.at[pl.ds(0, 2)], recv_sem.at[11])
        send(gathered.at[core], gathered.at[core], 13, (d ^ 1, c))
        for level, followers in [pair for pair in HAND_ON if pair[1]]:
            @pl.when(z == level)
            def _():
                for follower in followers:
                    send(gathered.at[core], gathered.at[core], 11, (half_x * 32 + follower * 2 + core, c))

        drained(gathered.at[1 - core], recv_sem.at[13])

    sides = [
        jnp.concatenate(
            [gathered[0, xx, 0:24], gathered[0, xx, 24:28], gathered[1, xx, 24:28], gathered[1, xx, 0:24]], axis=0
        )
        for xx in range(2)
    ]
    both = jnp.concatenate(sides, axis=1)
    high = both.astype(BF16)
    rest = both - high.astype(F32)
    mid = rest.astype(BF16)
    low = (rest - mid.astype(F32)).astype(BF16)
    split = jnp.concatenate([high.astype(F32), mid.astype(F32), low.astype(F32)], axis=0).astype(BF16)
    placed = jnp.dot(split, spread[...], preferred_element_type=F32)
    result = ((placed[0:56] + placed[56:112]) + placed[112:168]) * (1.0 / math.sqrt(ND * 32 * 128))
    for a in range(3):
        for b in range(3):
            for third in range(3):
                if third < 2:
                    t, part = 2 * a + third, b
                elif b < 2:
                    t, part = 2 * a + b, 3
                else:
                    t, part = 6, a
                filt_out[9 * a + 3 * b + third] = result[t * 8:t * 8 + 8, part * 64:part * 64 + 64]

    @pl.when(d == 0)
    def _():
        drained(seam_act, recv_sem.at[16])

    for group in (0, 1):
        drained(act_all.at[0], send_sem.at[group])
    drained(act_all.at[pl.ds(0, 2)], send_sem.at[2])
    for group in (12, 18, 20):
        drained(own, send_sem.at[group])
    drained(act_all.at[pl.ds(0, 3)], send_sem.at[4])
    drained(rows_recv.at[pl.ds(0, 15)], send_sem.at[5])
    drained(quad_recv.at[pl.ds(0, 3)], send_sem.at[6])
    drained(near_send.at[0], send_sem.at[9])
    drained(back_send.at[pl.ds(0, 120)], send_sem.at[10])

    @pl.when(seam)
    def _():
        drained(seam_recv.at[pl.ds(0, 15)], send_sem.at[15])

    @pl.when(jnp.logical_not(seam))
    def _():
        drained(own, send_sem.at[3])
        drained(own, send_sem.at[19])

    @pl.when(tail)
    def _():
        drained(seam_act, send_sem.at[16])

    @pl.when(jnp.logical_not(tail))
    def _():
        drained(near_send.at[1], send_sem.at[14])

    @pl.when(jnp.logical_and(z > 0, z < LATE))
    def _():
        drained(quarter, send_sem.at[7])

    @pl.when(z >= LATE)
    def _():
        drained(quarter, send_sem.at[8])

    @pl.when(owner)
    def _():
        drained(piece_recv.at[pl.ds(0, 3 + 2 * len(HAND_ON))], send_sem.at[11])

    @pl.when(jnp.logical_and(owner, goal != c))
    def _():
        drained(piece_recv.at[0], send_sem.at[11])

    @pl.when(jnp.logical_not(owner))
    def _():
        drained(gathered.at[0], send_sem.at[13])

    for level, followers in [pair for pair in HAND_ON if pair[1]]:
        @pl.when(z == level)
        def _():
            drained(piece_recv.at[pl.ds(0, 2 * len(followers))], send_sem.at[11])


def write_out(grad_in, filt_in, grad_out, filt_out):
    grad_out[...] = grad_in[...]
    filt_out[...] = filt_in[...]


def per_device(activations, slopes, weight):
    hbm = pl.BlockSpec(memory_space=pltpu.HBM)
    vmem = pl.BlockSpec(memory_space=pltpu.VMEM)
    grad, filt = pl.pallas_call(
        kernel,
        name="conv_grads",
        out_shape=(pltpu.VMEM((4, 32, 128), BF16), pltpu.VMEM((27, 8, 64), F32)),
        in_specs=[hbm] * 3,
        out_specs=(vmem, vmem),
        scratch_shapes=[
            pltpu.VMEM((8, 128, 128), BF16),
            pltpu.VMEM((8, 128, 128), BF16),
            pltpu.VMEM((160, 128), F32),
            pltpu.VMEM((6, 256, 128), BF16),
            pltpu.VMEM((27 * 64, 128), BF16),
            pltpu.VMEM((6 * 256 + 32, 128), F32),
            pltpu.VMEM((9 * 128, 128), F32),
            pltpu.VMEM((160, 32 * 128), BF16),
            pltpu.VMEM((96, 34 * 128), BF16),
            pltpu.VMEM((NC, 32, 128), BF16),
            pltpu.VMEM((NC, 32, 128), BF16),
            pltpu.VMEM((NC, 32, 128), BF16),
            pltpu.VMEM((NC, 32, 128), BF16),
            pltpu.VMEM((384, 512), BF16),
            pltpu.VMEM((2, 64, 256), F32),
            pltpu.VMEM((2, 64, 256), F32),
            pltpu.VMEM((64, 256), F32),
            pltpu.VMEM((128, 128), F32),
            pltpu.VMEM((136, 128), F32),
            pltpu.VMEM((NX, 2, 28, 128), F32),
            pltpu.VMEM((4, 28, 128), F32),
            pltpu.VMEM((28, 128), F32),
            pltpu.VMEM((NZ, 28, 128), F32),
            pltpu.VMEM((28, 128), F32),
            pltpu.VMEM((2, 2, 28, 128), F32),
            pltpu.VMEM((256, 256), BF16),
            pltpu.SemaphoreType.DMA((3,)),
            pltpu.SemaphoreType.DMA((21,)),
            pltpu.SemaphoreType.DMA((21,)),
        ],
        compiler_params=pltpu.CompilerParams(
            collective_id=0, has_side_effects=True, vmem_limit_bytes=32 * 1024 * 1024
        ),
    )(
        pltpu.with_memory_space_constraint(activations.reshape(128, 128), pltpu.HBM),
        pltpu.with_memory_space_constraint(slopes.reshape(256, 128), pltpu.HBM),
        pltpu.with_memory_space_constraint(weight.reshape(27 * 64, 128), pltpu.HBM),
    )
    grad, filt = pl.pallas_call(
        write_out,
        name="write_out",
        out_shape=(
            jax.ShapeDtypeStruct((4, 32, 128), BF16),
            jax.ShapeDtypeStruct((27, 8, 64), F32),
        ),
        in_specs=[vmem] * 2,
        out_specs=(vmem, vmem),
    )(pltpu.with_memory_space_constraint(grad, pltpu.VMEM), pltpu.with_memory_space_constraint(filt, pltpu.VMEM))
    return grad.reshape(4, 1, 32, 128), jnp.transpose(filt, (0, 2, 1))


def solution(mesh):
    placed = (P("chan", "depth", None, None), P("chan", "depth", None, None), P())
    return jax.shard_map(
        per_device,
        mesh=mesh,
        in_specs=placed,
        out_specs=(P("chan", "depth", None, None), P(None, None, "chan")),
        check_vma=False,
    )
```
